128 devices in a mesh: group: 4 (over x), sector: 32 (over y, z, core).
Axes of the slice: x: 4, y: 4, z: 4, core: 2. Of those that a mesh axis runs over, the one named last changes fastest.
Arguments:
- state: float32 [128, 128, 4, 128], P(('group', 'sector')), may hold values from -180 to 180
- panel: bfloat16 [32, 32, 256], P('group'), may hold values from -3 to 3
- left_env: bfloat16 [128, 32, 128, 128], P(('group', 'sector')), may hold values from -1.5 to 1.5
- right_env: bfloat16 [128, 32, 128, 128], P(('group', 'sector')), may hold values from -1 to 1
- left_match: int32 [128], P(('group', 'sector')), may hold values from 0 to 31
- right_match: int32 [128], P(('group', 'sector')), may hold values from 0 to 31
- phys_states: int32 [128, 4], P(('group', 'sector')), may hold values from 0 to 15, all different within a row
Outputs:
- new_state: float32 [128, 128, 4, 128], P(('group', 'sector'))
- hessenberg: float32 [8, 8], replicated
The draws below stay inside these ranges and needn't reach their ends.
Inputs may be any that keep to these rules, and one draw needn't show every extreme that they name: `left_match`: environment block index within the sector's own group, below 32. `right_match`: environment block index within the sector's own group, below 32. `phys_states`: each sector's 4 states are different.
All inputs are finite; a program needn't handle non-finite values.
Results may differ from the reference program's by a relative error of at most 0.025.
Values may be sent and summed in bfloat16 or wider, within the bound.
A program may use at most 128 MiB of HBM per device.

```python
import math
import jax
import jax.numpy as jnp
import numpy as np
from jax import lax

CHANNELS = 32
BLOCK = 128
PHYS = 4
LOCAL = 16
KRYLOV = 8
SECTORS = 128
ENV_GRP = 32


def draw_state(key, part):
    key = jax.random.fold_in(key, 11)
    first_key, row_key, col_key = jax.random.split(key, 3)
    shape = (SECTORS, BLOCK, PHYS, BLOCK)
    rising = 1.0 + 2.0 * jnp.arange(SECTORS, dtype=jnp.float32) / max(SECTORS - 1, 1)
    rising = rising.reshape(SECTORS, 1, 1, 1)
    row_scale = jnp.exp(jax.random.uniform(row_key, (SECTORS, BLOCK, 1, 1)) * math.log(10.0))
    col_scale = jnp.exp(jax.random.uniform(col_key, (SECTORS, 1, 1, BLOCK)) * math.log(10.0))
    base_draw = jnp.clip(jax.random.normal(first_key, shape), -6.0, 6.0)
    return (base_draw * rising * row_scale * col_scale / 10.0).astype(jnp.float32)


def unit_noise(key, shape, limit):
    return jnp.clip(jax.random.normal(key, shape), -limit, limit)


def draw_panel(key, part):
    key = jax.random.fold_in(key, 21)
    noise_key, jitter_key, repulse_key, chem_key = jax.random.split(key, 4)
    shape = (CHANNELS, CHANNELS, LOCAL * LOCAL)
    values = unit_noise(noise_key, shape, 6.0) * (CHANNELS * PHYS) ** (-0.5)
    repulsion = jax.random.uniform(repulse_key, (), minval=1.0, maxval=2.0)
    chemical = jax.random.uniform(chem_key, (), minval=0.4, maxval=0.8)
    site_state = jnp.arange(LOCAL, dtype=jnp.int32)
    first_site = site_state // 4
    second_site = site_state % 4
    filling = (first_site > 0).astype(jnp.float32) + (first_site == 3).astype(jnp.float32) + (second_site > 0).astype(jnp.float32) + (second_site == 3).astype(jnp.float32)
    doubles = (first_site == 3).astype(jnp.float32) + (second_site == 3).astype(jnp.float32)
    jitter = 0.2 * jnp.clip(jax.random.normal(jitter_key, (LOCAL,)), -3.0, 3.0)
    energy = repulsion * doubles - chemical * filling + jitter
    pair_ids = jnp.arange(LOCAL * LOCAL, dtype=jnp.int32)
    onsite = jnp.where(pair_ids // LOCAL == pair_ids % LOCAL, energy[pair_ids // LOCAL], 0.0)
    values = values.at[0, CHANNELS - 1].set(onsite)
    return values.astype(jnp.bfloat16)


def draw_left_env(key, part):
    key = jax.random.fold_in(key, 31)
    shape = (SECTORS, CHANNELS, BLOCK, BLOCK)
    values = unit_noise(key, shape, 4.0) * BLOCK ** (-0.5)
    identity = jnp.broadcast_to(jnp.eye(BLOCK, dtype=jnp.float32), (SECTORS, BLOCK, BLOCK))
    values = values.at[:, 0].set(identity)
    return values.astype(jnp.bfloat16)


def draw_right_env(key, part):
    key = jax.random.fold_in(key, 41)
    shape = (SECTORS, CHANNELS, BLOCK, BLOCK)
    values = unit_noise(key, shape, 6.0) * (CHANNELS * BLOCK) ** (-0.5)
    identity = jnp.broadcast_to(jnp.eye(BLOCK, dtype=jnp.float32), (SECTORS, BLOCK, BLOCK))
    values = values.at[:, CHANNELS - 1].set(identity)
    return values.astype(jnp.bfloat16)


def plant(array, own_key, smallest, high):
    dims = array.shape
    index_at = [jax.random.randint(jax.random.fold_in(own_key, axis), (), 0, dims[axis]) for axis in range(len(dims))]
    array = array.at[tuple(index_at)].set(smallest)
    longest = dims.index(max(dims))
    index_at[longest] = (index_at[longest] + 1) % dims[longest]
    return array.at[tuple(index_at)].set(high)


def rank_table(count, skew):
    weights = [(1 << 20) // math.isqrt(standing ** skew) + 1 for standing in range(1, count + 1)]
    width = 1 + sum(weights) // (1 << 30)
    return np.cumsum(np.array([max(1, weight // width) for weight in weights]))


def skewed_ids(rng, extent, number_of, lean):
    listing = rank_table(number_of, lean)
    ticket = jax.random.randint(jax.random.fold_in(rng, 1), extent, 0, int(listing[number_of - 1]))
    grade = jnp.searchsorted(jnp.asarray(listing, jnp.int32), ticket, side="right")
    return jax.random.permutation(jax.random.fold_in(rng, 2), number_of)[grade].astype(jnp.int32)


def choose_distinct(stream_key, rows, count, top, lift):
    order = jax.random.permutation(jax.random.fold_in(stream_key, 1), count)
    favour = order
    for power in range(3):
        favour = favour * favour // count
    favour = favour * lift // count
    chance = jax.random.randint(jax.random.fold_in(stream_key, 2), (rows, count), 0, 4096) + favour
    sure = jax.random.permutation(jax.random.fold_in(stream_key, 3), rows)[jnp.arange(count) % rows]
    chance = jnp.where(jnp.arange(rows)[:, None] == sure[None, :], 1 << 14, chance)
    priority = chance * count + jnp.arange(count)
    return lax.top_k(priority.astype(jnp.int32), top)[1].astype(jnp.int32)


def setup_inputs(seed: int = 0) -> dict:
    seeds = jax.random.split(jax.random.key(seed), 8)
    return {
        "state": draw_state(jax.random.fold_in(seeds[7], 71), 0),
        "panel": draw_panel(jax.random.fold_in(seeds[7], 71), 0),
        "left_env": draw_left_env(jax.random.fold_in(seeds[7], 71), 0),
        "right_env": draw_right_env(jax.random.fold_in(seeds[7], 71), 0),
        "left_match": plant(skewed_ids(seeds[4], (SECTORS,), ENV_GRP, 2), jax.random.fold_in(seeds[4], 3), 0, ENV_GRP - 1).astype(jnp.int32),
        "right_match": plant(skewed_ids(seeds[5], (SECTORS,), ENV_GRP, 1), jax.random.fold_in(seeds[5], 3), 0, ENV_GRP - 1).astype(jnp.int32),
        "phys_states": choose_distinct(seeds[6], SECTORS, LOCAL, PHYS, 0),
    }


TAU = 3.0
EPS = 1e-06
HIGH = lax.Precision.HIGHEST

def select_mix(panel, states):
    pairs = states[:, None] * 16 + states[None, :]
    choose = (jnp.arange(panel.shape[2], dtype=jnp.int32)[None, None, :] == pairs[:, :, None]).astype(jnp.float32)
    mixed = jnp.einsum('acz,qpz->aqcp', panel.astype(jnp.float32), choose, precision=HIGH)
    return mixed.astype(jnp.bfloat16)

def apply_sector(block_in, left_block, right_block, mixing):
    channels, size = (left_block.shape[0], left_block.shape[1])
    states = block_in.shape[1]
    inner = jnp.dot(left_block.reshape(channels * size, size), block_in.reshape(size, states * size), preferred_element_type=jnp.float32)
    inner = inner.astype(jnp.bfloat16).reshape(channels, size, states, size)
    middle = jnp.einsum('aiqj,aqcp->cipj', inner.astype(jnp.float32), mixing.astype(jnp.float32)).astype(jnp.bfloat16)
    return jnp.einsum('cipj,crj->ipr', middle.astype(jnp.float32), right_block.astype(jnp.float32))

def exponent_column(hessenberg):
    scaled = -TAU / 16.0 * hessenberg
    power_term = jnp.eye(hessenberg.shape[0], dtype=jnp.float32)
    series = power_term
    for order in range(1, 11):
        power_term = jnp.dot(power_term, scaled, precision=HIGH) / float(order)
        series = series + power_term
    for square in range(4):
        series = jnp.dot(series, series, precision=HIGH)
    return series[:, 0]

def reference(state, panel, left_env, right_env, left_match, right_match, phys_states):
    sector_ids = jnp.arange(SECTORS, dtype=jnp.int32)
    group_base = sector_ids // ENV_GRP * ENV_GRP
    left_ids = (group_base + left_match).astype(jnp.int32)
    right_ids = (group_base + right_match).astype(jnp.int32)
    mixes = jax.vmap(lambda states: select_mix(panel, states))(phys_states)

    def operate(vector):
        blocks = vector.reshape(SECTORS, BLOCK, PHYS, BLOCK).astype(jnp.bfloat16)

        def one_sector(pieces):
            block_in, left_id, right_id, mixing = pieces
            left_block = lax.dynamic_index_in_dim(left_env, left_id, 0, keepdims=False)
            right_block = lax.dynamic_index_in_dim(right_env, right_id, 0, keepdims=False)
            return apply_sector(block_in, left_block, right_block, mixing)
        return lax.map(one_sector, (blocks, left_ids, right_ids, mixes)).reshape(-1)
    flattened = state.reshape(-1)
    length = flattened.shape[0]
    start_sq = jnp.sum(flattened * flattened)
    krylov_basis = jnp.zeros((KRYLOV, length), jnp.float32).at[0].set(flattened / jnp.sqrt(start_sq + EPS))
    hessenberg = jnp.zeros((KRYLOV, KRYLOV), jnp.float32)
    for column in range(KRYLOV):
        applied = operate(krylov_basis[column])
        projection = jnp.dot(krylov_basis, applied, precision=HIGH)
        remainder = applied - jnp.dot(projection, krylov_basis, precision=HIGH)
        hessenberg = hessenberg.at[:, column].set(projection)
        if column + 1 < KRYLOV:
            subdiag = jnp.sqrt(jnp.sum(remainder * remainder) + EPS)
            hessenberg = hessenberg.at[column + 1, column].set(subdiag)
            krylov_basis = krylov_basis.at[column + 1].set(remainder / subdiag)
    coefficients = exponent_column(hessenberg)
    rescale = jnp.sqrt(jnp.float32(length)) / jnp.sqrt(jnp.sum(coefficients * coefficients))
    evolved = jnp.dot(coefficients, krylov_basis, precision=HIGH) * rescale
    return (evolved.reshape(state.shape), hessenberg)
```

```python
import functools

import jax
import jax.numpy as jnp
from jax import lax
from jax.experimental import pallas as pl
from jax.experimental.pallas import tpu as pltpu
from jax.sharding import PartitionSpec as P

MESH = pl.DeviceIdType.MESH
HIGH = lax.Precision.HIGHEST
F32 = jnp.float32
BF16 = jnp.bfloat16

KRYLOV = 8
TAU = 3.0
EPS = 1e-06
VMEM_LIMIT = 56 * 1024 * 1024


def route_kernel(
    lm_ref, rm_ref, panel_ref, left_ref, right_ref,
    left_out, right_out, panel_out,
    spread_l, spread_r, stage_l, stage_r, turned, match_v, match_s,
    send_l, recv_l, send_r, recv_r, send_l2, recv_l2, send_r2, recv_r2,
    send_m, recv_m, send_p, recv_p, own_sem,
):
    group = lax.axis_index("group")
    me = lax.axis_index("sector")
    groups = lax.axis_size("group")
    n = lax.axis_size("sector")

    barrier = pltpu.get_barrier_semaphore()

    def greet(k, _):
        pl.semaphore_signal(barrier, inc=1, device_id=(group, lax.rem(me + k, n)), device_id_type=MESH)
        return 0

    lax.fori_loop(1, n, greet, 0)
    for k in range(1, groups):
        pl.semaphore_signal(barrier, inc=1, device_id=(lax.rem(group + k, groups), me), device_id_type=MESH)

    lane = lax.broadcasted_iota(jnp.int32, (1, 128), 1)
    match_v[me] = jnp.where(lane == 0, lm_ref[0], rm_ref[0])
    own = [
        pltpu.make_async_copy(left_ref.at[me], spread_l.at[me], own_sem.at[0]),
        pltpu.make_async_copy(panel_ref, panel_out.at[group], own_sem.at[1]),
    ]
    for copy in own:
        copy.start()
    pl.semaphore_wait(barrier, n - 1 + groups - 1)

    def remote(src, dst, send, recv, peer):
        return pltpu.make_async_remote_copy(
            src_ref=src, dst_ref=dst, send_sem=send, recv_sem=recv, device_id=(group, peer), device_id_type=MESH
        )

    def spread_left(peer, slot):
        return remote(left_ref.at[peer], spread_l.at[slot], send_l.at[peer], recv_l.at[slot], peer)

    def spread_right(peer, slot):
        return remote(turned.at[peer], spread_r.at[slot], send_r.at[peer], recv_r.at[slot], peer)

    def tell(peer, slot):
        return remote(match_v.at[slot], match_v.at[slot], send_m.at[peer], recv_m.at[slot], peer)

    def route_left(peer, slot):
        return remote(stage_l.at[peer], left_out.at[slot], send_l2.at[peer], recv_l2.at[slot], peer)

    def route_right(peer, slot):
        return remote(stage_r.at[peer], right_out.at[slot], send_r2.at[peer], recv_r2.at[slot], peer)

    def panel_copy(k, slot):
        other = lax.rem(group + k, groups)
        return pltpu.make_async_remote_copy(
            src_ref=panel_ref, dst_ref=panel_out.at[slot], send_sem=send_p.at[other], recv_sem=recv_p.at[slot],
            device_id=(other, me), device_id_type=MESH,
        )

    def each_peer(body):
        def step(k, _):
            body(lax.rem(me + k, n))
            return 0

        lax.fori_loop(1, n, step, 0)

    def start_left(peer):
        tell(peer, me).start()
        spread_left(peer, me).start()

    each_peer(start_left)
    for k in range(1, groups):
        panel_copy(k, group).start()

    def turn(k, _):
        peer = lax.rem(me + k, n)
        turned[peer] = right_ref[peer].astype(F32).T.astype(BF16)

        @pl.when(k < n)
        def _():
            spread_right(peer, me).start()

        return 0

    lax.fori_loop(1, n + 1, turn, 0)
    spread_r[me] = turned[me]

    each_peer(lambda peer: tell(peer, peer).wait_recv())
    to_scalar = pltpu.make_async_copy(match_v, match_s, own_sem.at[2])
    to_scalar.start()
    own[0].wait()
    to_scalar.wait()
    each_peer(lambda peer: spread_left(peer, peer).wait_recv())

    def pick_left(peer):
        stage_l[peer] = spread_l[match_s[peer, 0, 0]]
        route_left(peer, me).start()

    each_peer(pick_left)
    stage_l[me] = spread_l[match_s[me, 0, 0]]
    keep_l = pltpu.make_async_copy(stage_l.at[me], left_out.at[me], own_sem.at[0])
    keep_l.start()

    each_peer(lambda peer: spread_right(peer, peer).wait_recv())

    def pick_right(peer):
        stage_r[peer] = spread_r[match_s[peer, 0, 1]]
        route_right(peer, me).start()

    each_peer(pick_right)
    stage_r[me] = spread_r[match_s[me, 0, 1]]
    keep_r = pltpu.make_async_copy(stage_r.at[me], right_out.at[me], own_sem.at[2])
    keep_r.start()

    own[1].wait()
    for k in range(1, groups):
        other = lax.rem(group + k, groups)
        panel_copy(k, other).wait_recv()
        panel_copy(k, group).wait_send()

    def finish(peer):
        tell(peer, me).wait_send()
        spread_left(peer, me).wait_send()
        spread_right(peer, me).wait_send()
        route_left(peer, me).wait_send()
        route_right(peer, me).wait_send()

    each_peer(finish)
    keep_l.wait()
    keep_r.wait()

    def arrived(peer):
        route_left(peer, peer).wait_recv()
        route_right(peer, peer).wait_recv()

    each_peer(arrived)


def route(left_match, right_match, panel, left_env, right_env, n, groups):
    channels, block = left_env.shape[1], left_env.shape[2]
    piece = (n, block, block)
    sems = [pltpu.SemaphoreType.DMA((n,))] * 10
    return pl.pallas_call(
        route_kernel,
        out_shape=(
            jax.ShapeDtypeStruct((channels, block, block), BF16),
            jax.ShapeDtypeStruct((channels, block, block), BF16),
            jax.ShapeDtypeStruct((groups,) + panel.shape, BF16),
        ),
        in_specs=[
            pl.BlockSpec(memory_space=pltpu.SMEM),
            pl.BlockSpec(memory_space=pltpu.SMEM),
            pl.BlockSpec(memory_space=pltpu.VMEM),
            pl.BlockSpec(memory_space=pltpu.VMEM),
            pl.BlockSpec(memory_space=pltpu.VMEM),
        ],
        out_specs=(
            pl.BlockSpec(memory_space=pltpu.VMEM),
            pl.BlockSpec(memory_space=pltpu.VMEM),
            pl.BlockSpec(memory_space=pltpu.VMEM),
        ),
        scratch_shapes=[pltpu.VMEM(piece, BF16)] * 5
        + [pltpu.VMEM((n, 1, 128), jnp.int32), pltpu.SMEM((n, 1, 128), jnp.int32)]
        + sems
        + [pltpu.SemaphoreType.DMA((groups,))] * 2
        + [pltpu.SemaphoreType.DMA((3,))],
        compiler_params=pltpu.CompilerParams(
            collective_id=0, has_side_effects=True, vmem_limit_bytes=VMEM_LIMIT
        ),
        name="route",
    )(left_match, right_match, panel, left_env[0], right_env[0])


def total(value):
    return jnp.sum(jnp.sum(value, axis=0, keepdims=True), axis=1, keepdims=True)


def fold(value):
    rows, columns = value.shape
    out = jnp.sum(value.reshape(rows // 8, 8, columns), axis=0)
    acc = out[:, :128]
    for start in range(128, columns, 128):
        acc = acc + out[:, start : start + 128]
    return acc


def sector_kernel(states_ref, state_ref, panel_ref, left_ref, right_ref, basis_ref, row_ref, chosen, spread, rt32, joint, z, x, y):
    channels, block = left_ref.shape[0], left_ref.shape[1]
    phys = states_ref.shape[1]
    wide = phys * block
    lane = lax.broadcasted_iota(jnp.int32, (1, 128), 1)

    pick = lax.broadcasted_iota(jnp.int32, (16, 256), 0)
    want = jnp.zeros((16, 256), jnp.int32)
    for p in range(phys):
        for q in range(phys):
            want = jnp.where(pick == p * phys + q, 16 * states_ref[0, q] + states_ref[0, p], want)
    choose = (want == lax.broadcasted_iota(jnp.int32, (16, 256), 1)).astype(BF16)
    chosen[...] = lax.dot_general(
        choose, panel_ref[...], (((1,), (1,)), ((), ())), preferred_element_type=F32
    )

    grow = (
        lax.broadcasted_iota(jnp.int32, (channels, 8 * channels), 0)
        == lax.broadcasted_iota(jnp.int32, (channels, 8 * channels), 1) // 8
    ).astype(BF16)
    same = lax.broadcasted_iota(jnp.int32, (1, 8, 8 * channels), 1) == lax.rem(
        lax.broadcasted_iota(jnp.int32, (1, 8, 8 * channels), 2), 8
    )
    for p in range(phys):
        rows = jnp.concatenate(
            [chosen[p * phys : (p + 1) * phys, a * channels : (a + 1) * channels] for a in range(channels)], axis=0
        )
        grown = jnp.dot(rows.astype(BF16), grow, preferred_element_type=F32)
        spread[p] = (
            jnp.where(same, grown[:, None, :], 0.0).reshape(channels * phys * 8, 8 * channels).astype(BF16)
        )

    def widen(c, _):
        rt32[c] = right_ref[c].astype(F32)
        return 0

    lax.fori_loop(0, channels, widen, 0)

    def join(m, _):
        start = pl.multiple_of(m * 16, 16)
        upper = rt32[:, pl.ds(start, 8), :].reshape(channels * 8, block)
        lower = rt32[:, pl.ds(start + 8, 8), :].reshape(channels * 8, block)
        both = jnp.concatenate([upper, lower], axis=1).astype(BF16)
        for p in range(phys):
            out = jnp.dot(spread[p], both, preferred_element_type=F32)
            tiles = out.reshape(channels * phys, 8, 2 * block)
            joint[:, pl.ds(start, 16), p * block : (p + 1) * block] = jnp.concatenate(
                [tiles[:, :, :block], tiles[:, :, block:]], axis=1
            ).astype(BF16)
        return 0

    lax.fori_loop(0, block // 16, join, 0)

    big = jnp.max(jnp.max(jnp.abs(state_ref[...]), axis=0, keepdims=True), axis=1, keepdims=True)
    shrink = jnp.where(big > 0.0, 1.0 / big, 0.0)
    for q in range(phys):
        part = state_ref[pl.ds(q, block, stride=phys), :] * shrink
        basis_ref[0, :, q * block : (q + 1) * block] = part
    size = jnp.sqrt(total(fold(basis_ref[0] * basis_ref[0])))
    first = basis_ref[0] * jnp.where(size > 0.0, 1.0 / size, 0.0)
    basis_ref[0] = first
    x[...] = first.astype(BF16)
    for j in range(1, KRYLOV):
        basis_ref[j] = jnp.zeros((block, wide), F32)
    row = jnp.where(lane == 64, big * size, 0.0)

    def apply():
        def left(a, _):
            z[a] = jnp.dot(left_ref[a], x[...], preferred_element_type=F32).astype(BF16)
            return 0

        lax.fori_loop(0, channels, left, 0, unroll=4)
        y[...] = jnp.zeros_like(y)

        def right(a, _):
            weights = joint[pl.ds(pl.multiple_of(a * phys, phys), phys)].reshape(phys * block, wide)
            y[...] += jnp.dot(z[a], weights, preferred_element_type=F32)
            return 0

        lax.fori_loop(0, channels, right, 0, unroll=4)

    for t in range(KRYLOV):
        apply()
        applied = y[...]
        heights = [total(fold(basis_ref[j] * applied)) for j in range(t + 1)]
        for j in range(t + 1):
            row = jnp.where(lane == t * KRYLOV + j, heights[j], row)
        if t + 1 < KRYLOV:
            rest = applied
            for j in range(t + 1):
                rest = rest - heights[j] * basis_ref[j]
            square = total(fold(rest * rest))
            scale = jnp.where(square > 0.0, lax.rsqrt(square), 0.0)
            new = rest * scale
            basis_ref[t + 1] = new
            x[...] = new.astype(BF16)
            row = jnp.where(lane == t * KRYLOV + t + 1, square * scale, row)
    row_ref[...] = row


def sector(states, state, panel, left, right):
    channels, block = left.shape[0], left.shape[1]
    phys = states.shape[1]
    wide = phys * block
    vmem = pl.BlockSpec(memory_space=pltpu.VMEM)
    return pl.pallas_call(
        sector_kernel,
        out_shape=(
            jax.ShapeDtypeStruct((KRYLOV, block, wide), F32),
            jax.ShapeDtypeStruct((1, 128), F32),
        ),
        in_specs=[pl.BlockSpec(memory_space=pltpu.SMEM), vmem, vmem, vmem, vmem],
        out_specs=(vmem, vmem),
        scratch_shapes=[
            pltpu.VMEM((phys * phys, channels * channels), F32),
            pltpu.VMEM((phys, channels * phys * 8, channels * 8), BF16),
            pltpu.VMEM((channels, block, block), F32),
            pltpu.VMEM((channels * phys, block, wide), BF16),
            pltpu.VMEM((channels, block, wide), BF16),
            pltpu.VMEM((block, wide), BF16),
            pltpu.VMEM((block, wide), F32),
        ],
        compiler_params=pltpu.CompilerParams(vmem_limit_bytes=VMEM_LIMIT),
        name="sector",
    )(states, state, panel, left, right)


def multiply(a, b):
    out = a[:, 0:1] * b[0:1, :]
    for k in range(1, KRYLOV):
        out = out + a[:, k : k + 1] * b[k : k + 1, :]
    return out


def joint_kernel(row_ref, hess_ref, weight_ref, table, send_a, recv_a, send_b, recv_b):
    group = lax.axis_index("group")
    me = lax.axis_index("sector")
    groups = lax.axis_size("group")
    n = lax.axis_size("sector")
    near = 8
    lines = n // near
    line, place = me // near, lax.rem(me, near)
    home = group * lines + line

    def next_near(k):
        return (group, line * near + lax.rem(place + k, near))

    def next_far(k):
        other = lax.rem(home + k, groups * lines)
        return (other // lines, lax.rem(other, lines) * near + place)

    barrier = pltpu.get_barrier_semaphore()
    for k in range(1, near):
        pl.semaphore_signal(barrier, inc=1, device_id=next_near(k), device_id_type=MESH)
    for k in range(1, groups * lines):
        pl.semaphore_signal(barrier, inc=1, device_id=next_far(k), device_id_type=MESH)
    table[home, pl.ds(place, 1), :] = row_ref[...]
    pl.semaphore_wait(barrier, near - 1 + groups * lines - 1)

    def near_copy(k, slot):
        piece = table.at[home, pl.ds(slot, 1), :]
        return pltpu.make_async_remote_copy(
            src_ref=piece, dst_ref=piece, send_sem=send_a.at[k], recv_sem=recv_a.at[slot],
            device_id=next_near(k), device_id_type=MESH,
        )

    def far_copy(k, slot):
        piece = table.at[slot]
        return pltpu.make_async_remote_copy(
            src_ref=piece, dst_ref=piece, send_sem=send_b.at[k], recv_sem=recv_b.at[slot],
            device_id=next_far(k), device_id_type=MESH,
        )

    for k in range(1, near):
        near_copy(k, place).start()
    for k in range(1, near):
        near_copy(k, lax.rem(place + k, near)).wait_recv()
    for k in range(1, groups * lines):
        far_copy(k, home).start()
    for k in range(1, groups * lines):
        far_copy(k, lax.rem(home + k, groups * lines)).wait_recv()

    entries = table[...].reshape(groups * n, 128).T
    columns = [entries[t * KRYLOV : (t + 1) * KRYLOV, :] for t in range(KRYLOV)]
    norms = entries[64:65, :]
    sub = lax.broadcasted_iota(jnp.int32, (KRYLOV, 128), 0)
    lane = lax.broadcasted_iota(jnp.int32, (KRYLOV, 128), 1)

    start_sq = total(norms * norms)
    vectors = [jnp.where(sub == 0, norms / jnp.sqrt(start_sq + EPS), 0.0)]
    hess = jnp.zeros((KRYLOV, 128), F32)
    for t in range(KRYLOV):
        now = vectors[t]
        applied = columns[0] * now[0:1, :]
        for i in range(1, t + 1):
            applied = applied + columns[i] * now[i : i + 1, :]
        heights = [total(vectors[j] * applied) for j in range(t + 1)]
        for j in range(t + 1):
            hess = jnp.where((sub == j) & (lane == t), heights[j], hess)
        if t + 1 < KRYLOV:
            rest = applied
            for j in range(t + 1):
                rest = rest - heights[j] * vectors[j]
            beta = jnp.sqrt(total(rest * rest) + EPS)
            hess = jnp.where((sub == t + 1) & (lane == t), beta, hess)
            vectors.append(rest / beta)

    scaled = (-TAU / 16.0) * hess
    power = jnp.where(sub == lane, 1.0, 0.0).astype(F32)
    series = power
    for order in range(1, 11):
        power = multiply(power, scaled) / float(order)
        series = series + power
    for _ in range(4):
        series = multiply(series, series)
    coefficients = series[:, 0:1]
    entries_total = float(groups * n * 128 * 4 * 128)
    rescale = jnp.sqrt(jnp.full((1, 1), entries_total, F32)) / jnp.sqrt(
        jnp.sum(coefficients * coefficients, axis=0, keepdims=True)
    )
    mixed = coefficients[0:1, :] * vectors[0]
    for t in range(1, KRYLOV):
        mixed = mixed + coefficients[t : t + 1, :] * vectors[t]
    mine = jnp.sum(jnp.where(lane == group * n + me, mixed, 0.0), axis=1, keepdims=True)
    hess_ref[...] = hess[:, :KRYLOV]
    weight_ref[...] = jnp.broadcast_to(mine * rescale, (KRYLOV, 128))

    for k in range(1, near):
        near_copy(k, place).wait_send()
    for k in range(1, groups * lines):
        far_copy(k, home).wait_send()


def join_sectors(row, n, groups):
    vmem = pl.BlockSpec(memory_space=pltpu.VMEM)
    lines = n // 8
    return pl.pallas_call(
        joint_kernel,
        out_shape=(
            jax.ShapeDtypeStruct((KRYLOV, KRYLOV), F32),
            jax.ShapeDtypeStruct((KRYLOV, 128), F32),
        ),
        in_specs=[vmem],
        out_specs=(vmem, vmem),
        scratch_shapes=[
            pltpu.VMEM((groups * lines, 8, 128), F32),
            pltpu.SemaphoreType.DMA((8,)),
            pltpu.SemaphoreType.DMA((8,)),
            pltpu.SemaphoreType.DMA((groups * lines,)),
            pltpu.SemaphoreType.DMA((groups * lines,)),
        ],
        compiler_params=pltpu.CompilerParams(collective_id=1, has_side_effects=True),
        name="joint",
    )(row)


def evolve_kernel(basis_ref, weight_ref, out_ref):
    phys = basis_ref.shape[2] // 128
    block = basis_ref.shape[1]
    for p in range(phys):
        acc = weight_ref[0:1, :] * basis_ref[0, :, p * 128 : (p + 1) * 128]
        for j in range(1, KRYLOV):
            acc = acc + weight_ref[j : j + 1, :] * basis_ref[j, :, p * 128 : (p + 1) * 128]
        out_ref[pl.ds(p, block, stride=phys), :] = acc


def evolve(basis, weight):
    vmem = pl.BlockSpec(memory_space=pltpu.VMEM)
    block, wide = basis.shape[1], basis.shape[2]
    return pl.pallas_call(
        evolve_kernel,
        out_shape=jax.ShapeDtypeStruct((block * wide // 128, 128), F32),
        in_specs=[vmem, vmem],
        out_specs=vmem,
        compiler_params=pltpu.CompilerParams(vmem_limit_bytes=VMEM_LIMIT),
        name="evolve",
    )(basis, weight)


def local(state, panel, left_env, right_env, left_match, right_match, phys_states):
    n, groups = lax.axis_size("sector"), lax.axis_size("group")
    left, right, full_panel = route(left_match, right_match, panel, left_env, right_env, n, groups)
    channels = left.shape[0]
    flat_panel = full_panel.reshape(channels * full_panel.shape[2], full_panel.shape[3])
    rows = state.reshape(-1, state.shape[-1])
    basis, row = sector(phys_states, rows, flat_panel, left, right)
    hess, weight = join_sectors(row, n, groups)
    return evolve(basis, weight).reshape(state.shape), hess


def solution(mesh):
    return jax.shard_map(
        local,
        mesh=mesh,
        in_specs=(
            P(("group", "sector"), None, None, None),
            P("group", None, None),
            P(("group", "sector"), None, None, None),
            P(("group", "sector"), None, None, None),
            P(("group", "sector")),
            P(("group", "sector")),
            P(("group", "sector"), None),
        ),
        out_specs=(P(("group", "sector"), None, None, None), P()),
        check_vma=False,
    )
```

```python
import functools

import jax
import jax.numpy as jnp
from jax import lax
from jax.experimental import pallas as pl
from jax.experimental.pallas import tpu as pltpu
from jax.sharding import PartitionSpec as P

MESH = pl.DeviceIdType.MESH
F32 = jnp.float32
BF16 = jnp.bfloat16

KRYLOV = 8
TAU = 3.0
EPS = 1e-06
VMEM_LIMIT = 56 * 1024 * 1024
SIDE = 4
HALVES = 2


def far_first():
    def away(offset):
        return min(offset[0], SIDE - offset[0]) + min(offset[1], SIDE - offset[1])

    every = [(y, z, c) for y in range(SIDE) for z in range(SIDE) for c in range(2)]
    order = []
    for offset in sorted(every[1:], key=lambda o: -away(o)):
        for _ in range(4):
            if offset not in order and offset in every[1:]:
                order.append(offset)
            offset = (offset[1], (SIDE - offset[0]) % SIDE, offset[2])
    return order


ORDER = far_first()


def total(value):
    return jnp.sum(jnp.sum(value, axis=0, keepdims=True), axis=1, keepdims=True)


def narrow(value):
    return (value[:, :128] + value[:, 128:256]) + (value[:, 256:384] + value[:, 384:])


def multiply(a, b):
    out = a[:, 0:1] * b[0:1, :]
    for k in range(1, KRYLOV):
        out = out + a[:, k : k + 1] * b[k : k + 1, :]
    return out


def kernel(
    lm_ref, rm_ref, states_ref, state_ref, panel_ref, left_ref, right_ref,
    out_ref, hess_ref,
    right_v, turned, spread_l, spread_r, stage_l, stage_r, left_in, right_in, match_v, match_s, panels,
    chosen, grown, joint, left_w, z, x, y, basis, row_ref, table,
    own_sem, send_m, recv_m, send_l, recv_l, send_r, recv_r, send_l2, recv_l2, send_r2, recv_r2,
    send_p, recv_p, send_a, recv_a, send_b, recv_b, send_c, recv_c,
):
    group = lax.axis_index("group")
    me = lax.axis_index("sector")
    groups = lax.axis_size("group")
    n = lax.axis_size("sector")
    near = 2 * SIDE
    line, place = me // near, lax.rem(me, near)
    chip, core = lax.rem(me // 2, SIDE), lax.rem(me, 2)
    channels, block = left_in.shape[0], left_in.shape[1]
    phys = states_ref.shape[1]
    wide = phys * block

    def at(offset):
        dy, dz, dc = offset
        return lax.rem(line + dy, SIDE) * near + lax.rem(chip + dz, SIDE) * 2 + lax.rem(core + dc, 2)

    def each_peer(body):
        def step(k, _):
            body(lax.rem(me + k, n))
            return 0

        lax.fori_loop(1, n, step, 0)

    barrier = pltpu.get_barrier_semaphore()
    each_peer(lambda peer: pl.semaphore_signal(barrier, inc=1, device_id=(group, peer), device_id_type=MESH))
    for k in range(1, groups):
        pl.semaphore_signal(barrier, inc=1, device_id=(lax.rem(group + k, groups), me), device_id_type=MESH)

    load_r = pltpu.make_async_copy(right_ref, right_v, own_sem.at[0])
    keep_l = pltpu.make_async_copy(left_ref.at[me], spread_l.at[me], own_sem.at[1])
    load_r.start()
    keep_l.start()
    panels[group] = panel_ref[...]
    lane = lax.broadcasted_iota(jnp.int32, (1, 128), 1)
    match_v[me] = jnp.where(lane == 0, lm_ref[0], rm_ref[0])
    pl.semaphore_wait(barrier, n - 1 + groups - 1)

    def remote(src, dst, send, recv, device):
        return pltpu.make_async_remote_copy(
            src_ref=src, dst_ref=dst, send_sem=send, recv_sem=recv, device_id=device, device_id_type=MESH
        )

    def tell(peer, slot):
        return remote(match_v.at[slot], match_v.at[slot], send_m.at[peer], recv_m.at[slot], (group, peer))

    def spread_left(peer, slot):
        return remote(left_ref.at[peer], spread_l.at[slot], send_l.at[peer], recv_l.at[slot], (group, peer))

    def spread_right(peer, slot):
        return remote(turned.at[peer], spread_r.at[slot], send_r.at[peer], recv_r.at[slot], (group, peer))

    def route_left(peer, slot):
        return remote(stage_l.at[peer], left_in.at[slot], send_l2.at[peer], recv_l2.at[slot], (group, peer))

    part = block // HALVES

    def route_right(h, peer, slot):
        rows = pl.ds(h * part, part)
        return remote(
            stage_r.at[peer, rows], right_in.at[slot, rows], send_r2.at[h, peer], recv_r2.at[h, slot], (group, peer)
        )

    def panel_copy(k, slot):
        other = lax.rem(group + k, groups)
        return remote(panels.at[slot], panels.at[slot], send_p.at[other], recv_p.at[slot], (other, me))

    for offset in ORDER:
        tell(at(offset), me).start()
    for offset in ORDER:
        spread_left(at(offset), me).start()
    for k in range(1, groups):
        panel_copy(k, group).start()
    load_r.wait()

    def turn(peer):
        turned[peer] = right_v[peer].astype(F32).T.astype(BF16)

    for offset in ORDER:
        peer = at(offset)
        turn(peer)
        spread_right(peer, me).start()
    spread_r[me] = right_v[me].astype(F32).T.astype(BF16)

    big = jnp.max(jnp.max(jnp.abs(state_ref[...]), axis=0, keepdims=True), axis=1, keepdims=True)
    shrink = jnp.where(big > 0.0, 1.0 / big, 0.0)
    for q in range(phys):
        y[:, q * block : (q + 1) * block] = state_ref[pl.ds(q, block, stride=phys), :] * shrink
    acc = jnp.zeros((8, 128), F32)
    for r in range(0, block, 8):
        piece = y[r : r + 8, :]
        acc = acc + narrow(piece * piece)
    size = jnp.sqrt(total(acc))
    scale = jnp.where(size > 0.0, 1.0 / size, 0.0)
    for r in range(0, block, 16):
        first = y[r : r + 16, :] * scale
        basis[0, r : r + 16, :] = first
        x[r : r + 16, :] = first.astype(BF16)
    row_ref[...] = jnp.where(lane == 64, big * size, 0.0)

    for k in range(1, groups):
        panel_copy(k, lax.rem(group + k, groups)).wait_recv()
    pick = lax.broadcasted_iota(jnp.int32, (16, 256), 0)
    want = jnp.zeros((16, 256), jnp.int32)
    for p in range(phys):
        for q in range(phys):
            want = jnp.where(pick == p * phys + q, 16 * states_ref[0, q] + states_ref[0, p], want)
    choose = (want == lax.broadcasted_iota(jnp.int32, (16, 256), 1)).astype(BF16)
    chosen[...] = lax.dot_general(
        choose,
        panels[...].reshape(channels * channels, 256),
        (((1,), (1,)), ((), ())),
        preferred_element_type=F32,
    )
    grow = (
        lax.broadcasted_iota(jnp.int32, (channels, 8 * channels), 0)
        == lax.broadcasted_iota(jnp.int32, (channels, 8 * channels), 1) // 8
    ).astype(BF16)
    same = lax.broadcasted_iota(jnp.int32, (1, 8, 8 * channels), 1) == lax.rem(
        lax.broadcasted_iota(jnp.int32, (1, 8, 8 * channels), 2), 8
    )
    for p in range(phys):
        rows = jnp.concatenate(
            [chosen[p * phys : (p + 1) * phys, a * channels : (a + 1) * channels] for a in range(channels)], axis=0
        )
        wider = jnp.dot(rows.astype(BF16), grow, preferred_element_type=F32)
        grown[p] = jnp.where(same, wider[:, None, :], 0.0).reshape(channels * phys * 8, 8 * channels).astype(BF16)

    each_peer(lambda peer: tell(peer, peer).wait_recv())
    to_scalar = pltpu.make_async_copy(match_v, match_s, own_sem.at[2])
    to_scalar.start()
    keep_l.wait()
    to_scalar.wait()
    each_peer(lambda peer: spread_left(peer, peer).wait_recv())
    for offset in ORDER:
        peer = at(offset)
        stage_l[peer] = spread_l[match_s[peer, 0, 0]]
        route_left(peer, me).start()
    left_in[me] = spread_l[match_s[me, 0, 0]]

    each_peer(lambda peer: spread_right(peer, peer).wait_recv())
    for h in range(HALVES):
        for offset in ORDER:
            peer = at(offset)
            if h == 0:
                stage_r[peer] = spread_r[match_s[peer, 0, 1]]
            route_right(h, peer, me).start()
    right_in[me] = spread_r[match_s[me, 0, 1]]

    each_peer(lambda peer: route_left(peer, peer).wait_recv())
    for a in range(channels):
        left_w[:, a * block : (a + 1) * block] = left_in[a]

    def join(m, _):
        start = pl.multiple_of(m * 16, 16)
        lines_in = right_in[:, pl.ds(start, 16), :].astype(F32)
        both = jnp.concatenate(
            [lines_in[:, :8].reshape(channels * 8, block), lines_in[:, 8:].reshape(channels * 8, block)], axis=1
        ).astype(BF16)
        for p in range(phys):
            out = jnp.dot(grown[p], both, preferred_element_type=F32)
            tiles = out.reshape(channels * phys, 8, 2 * block)
            joint[:, pl.ds(start, 16), p * block : (p + 1) * block] = jnp.concatenate(
                [tiles[:, :, :block], tiles[:, :, block:]], axis=1
            ).astype(BF16)
        return 0

    for h in range(HALVES):
        each_peer(lambda peer: route_right(h, peer, peer).wait_recv())
        lax.fori_loop(h * part // 16, (h + 1) * part // 16, join, 0)

    def apply():
        for a in range(channels):
            weights = joint[a * phys : (a + 1) * phys].reshape(wide, wide)
            z[a] = jnp.dot(x[...], weights, preferred_element_type=F32).astype(BF16)
        y[...] = jnp.dot(left_w[...], z[...].reshape(channels * block, wide), preferred_element_type=F32)

    def orthogonalize(t):
        accs = [jnp.zeros((8, 128), F32)] * (t + 1)
        for r in range(0, block, 8):
            piece = y[r : r + 8, :]
            for j in range(t + 1):
                accs[j] = accs[j] + narrow(basis[j, r : r + 8, :] * piece)
        heights = [total(acc) for acc in accs]
        row = row_ref[...]
        for j in range(t + 1):
            row = jnp.where(lane == t * KRYLOV + j, heights[j], row)
        if t + 1 < KRYLOV:
            acc = jnp.zeros((8, 128), F32)
            for r in range(0, block, 8):
                rest = y[r : r + 8, :]
                for j in range(t + 1):
                    rest = rest - heights[j] * basis[j, r : r + 8, :]
                y[r : r + 8, :] = rest
                acc = acc + narrow(rest * rest)
            square = total(acc)
            scale = jnp.where(square > 0.0, lax.rsqrt(square), 0.0)
            for r in range(0, block, 16):
                new = y[r : r + 16, :] * scale
                basis[t + 1, r : r + 16, :] = new
                x[r : r + 16, :] = new.astype(BF16)
            row = jnp.where(lane == t * KRYLOV + t + 1, square * scale, row)
        row_ref[...] = row

    def krylov_step(t, _):
        apply()
        for i in range(KRYLOV):
            pl.when(t == i)(functools.partial(orthogonalize, i))
        return 0

    lax.fori_loop(0, KRYLOV, krylov_step, 0)

    home = group * SIDE + line
    table[home, pl.ds(place, 1), :] = row_ref[...]

    def copy_a(k, slot):
        piece = table.at[home, pl.ds(slot, 1), :]
        other = line * near + lax.rem(place + k, near)
        return remote(piece, piece, send_a.at[k], recv_a.at[slot], (group, other))

    def copy_b(k, slot):
        piece = table.at[group * SIDE + slot]
        other = lax.rem(line + k, SIDE) * near + place
        return remote(piece, piece, send_b.at[k], recv_b.at[slot], (group, other))

    def copy_c(k, slot):
        piece = table.at[pl.ds(slot * SIDE, SIDE)]
        return remote(piece, piece, send_c.at[k], recv_c.at[slot], (lax.rem(group + k, groups), me))

    for k in range(1, near):
        copy_a(k, place).start()
    for k in range(1, near):
        copy_a(k, lax.rem(place + k, near)).wait_recv()
    for k in range(1, SIDE):
        copy_b(k, line).start()
    for k in range(1, SIDE):
        copy_b(k, lax.rem(line + k, SIDE)).wait_recv()
    for k in range(1, groups):
        copy_c(k, group).start()
    for k in range(1, groups):
        copy_c(k, lax.rem(group + k, groups)).wait_recv()

    entries = table[...].reshape(groups * n, 128).T
    columns = [entries[t * KRYLOV : (t + 1) * KRYLOV, :] for t in range(KRYLOV)]
    norms = entries[64:65, :]
    sub = lax.broadcasted_iota(jnp.int32, (KRYLOV, 128), 0)
    lanes = lax.broadcasted_iota(jnp.int32, (KRYLOV, 128), 1)
    vectors = [jnp.where(sub == 0, norms / jnp.sqrt(total(norms * norms) + EPS), 0.0)]
    hess = jnp.zeros((KRYLOV, 128), F32)
    for t in range(KRYLOV):
        now = vectors[t]
        applied = columns[0] * now[0:1, :]
        for i in range(1, t + 1):
            applied = applied + columns[i] * now[i : i + 1, :]
        heights = [total(vectors[j] * applied) for j in range(t + 1)]
        for j in range(t + 1):
            hess = jnp.where((sub == j) & (lanes == t), heights[j], hess)
        if t + 1 < KRYLOV:
            rest = applied
            for j in range(t + 1):
                rest = rest - heights[j] * vectors[j]
            beta = jnp.sqrt(total(rest * rest) + EPS)
            hess = jnp.where((sub == t + 1) & (lanes == t), beta, hess)
            vectors.append(rest / beta)
    hess_ref[...] = hess[:, :KRYLOV]

    scaled = (-TAU / 16.0) * hess
    power = jnp.where(sub == lanes, 1.0, 0.0).astype(F32)
    series = power
    for order in range(1, 11):
        power = multiply(power, scaled) / float(order)
        series = series + power
    for _ in range(4):
        series = multiply(series, series)
    coefficients = series[:, 0:1]
    length = float(groups * n * block * wide)
    rescale = jnp.sqrt(jnp.full((1, 1), length, F32)) / jnp.sqrt(
        jnp.sum(coefficients * coefficients, axis=0, keepdims=True)
    )
    mixed = coefficients[0:1, :] * vectors[0]
    for t in range(1, KRYLOV):
        mixed = mixed + coefficients[t : t + 1, :] * vectors[t]
    weight = jnp.sum(jnp.where(lanes == group * n + me, mixed, 0.0), axis=1, keepdims=True) * rescale
    for p in range(phys):
        columns_p = slice(p * block, (p + 1) * block)
        acc = weight[0:1, :] * basis[0, :, columns_p]
        for j in range(1, KRYLOV):
            acc = acc + weight[j : j + 1, :] * basis[j, :, columns_p]
        out_ref[pl.ds(p, block, stride=phys), :] = acc

    def finish(peer):
        tell(peer, me).wait_send()
        spread_left(peer, me).wait_send()
        spread_right(peer, me).wait_send()
        route_left(peer, me).wait_send()
        for h in range(HALVES):
            route_right(h, peer, me).wait_send()

    each_peer(finish)
    for k in range(1, groups):
        panel_copy(k, group).wait_send()
        copy_c(k, group).wait_send()
    for k in range(1, SIDE):
        copy_b(k, line).wait_send()
    for k in range(1, near):
        copy_a(k, place).wait_send()


def local(state, panel, left_env, right_env, left_match, right_match, phys_states):
    n, groups = lax.axis_size("sector"), lax.axis_size("group")
    channels, block = left_env.shape[1], left_env.shape[2]
    phys = phys_states.shape[1]
    wide = phys * block
    rows = state.reshape(-1, state.shape[-1])
    vmem = pl.BlockSpec(memory_space=pltpu.VMEM)
    smem = pl.BlockSpec(memory_space=pltpu.SMEM)
    whole = pl.BlockSpec(memory_space=pl.ANY)
    piece = (n, block, block)
    dma = pltpu.SemaphoreType.DMA
    new_state, hessenberg = pl.pallas_call(
        kernel,
        out_shape=(
            jax.ShapeDtypeStruct(rows.shape, F32),
            jax.ShapeDtypeStruct((KRYLOV, KRYLOV), F32),
        ),
        in_specs=[smem, smem, smem, vmem, vmem, whole, whole],
        out_specs=(vmem, vmem),
        scratch_shapes=[
            pltpu.VMEM(piece, BF16),
            pltpu.VMEM(piece, BF16),
            pltpu.VMEM(piece, BF16),
            pltpu.VMEM(piece, BF16),
            pltpu.VMEM(piece, BF16),
            pltpu.VMEM(piece, BF16),
            pltpu.VMEM(piece, BF16),
            pltpu.VMEM(piece, BF16),
            pltpu.VMEM((n, 1, 128), jnp.int32),
            pltpu.SMEM((n, 1, 128), jnp.int32),
            pltpu.VMEM((groups,) + panel.shape, BF16),
            pltpu.VMEM((phys * phys, channels * channels), F32),
            pltpu.VMEM((phys, channels * phys * 8, channels * 8), BF16),
            pltpu.VMEM((channels * phys, block, wide), BF16),
            pltpu.VMEM((block, channels * block), BF16),
            pltpu.VMEM((channels, block, wide), BF16),
            pltpu.VMEM((block, wide), BF16),
            pltpu.VMEM((block, wide), F32),
            pltpu.VMEM((KRYLOV, block, wide), F32),
            pltpu.VMEM((1, 128), F32),
            pltpu.VMEM((groups * SIDE, 2 * SIDE, 128), F32),
            dma((3,)),
        ]
        + [dma((n,))] * 8
        + [dma((HALVES, n))] * 2
        + [dma((groups,))] * 2
        + [dma((2 * SIDE,))] * 2
        + [dma((SIDE,))] * 2
        + [dma((groups,))] * 2,
        compiler_params=pltpu.CompilerParams(collective_id=0, has_side_effects=True, vmem_limit_bytes=VMEM_LIMIT),
        name="step",
    )(left_match, right_match, phys_states, rows, panel, left_env[0], right_env[0])
    return new_state.reshape(state.shape), hessenberg


def solution(mesh):
    return jax.shard_map(
        local,
        mesh=mesh,
        in_specs=(
            P(("group", "sector"), None, None, None),
            P("group", None, None),
            P(("group", "sector"), None, None, None),
            P(("group", "sector"), None, None, None),
            P(("group", "sector")),
            P(("group", "sector")),
            P(("group", "sector"), None),
        ),
        out_specs=(P(("group", "sector"), None, None, None), P()),
        check_vma=False,
    )
```

```python
import functools
import math

import jax
import jax.numpy as jnp
from jax import lax
from jax.experimental import pallas as pl
from jax.experimental.pallas import tpu as pltpu
from jax.sharding import PartitionSpec as P

MESH = pl.DeviceIdType.MESH
F32 = jnp.float32
BF16 = jnp.bfloat16

KRYLOV = 8
TAU = 3.0
EPS = 1e-06
VMEM_LIMIT = 56 * 1024 * 1024
SIDE = 4


def far_first():
    def away(offset):
        return min(offset[0], SIDE - offset[0]) + min(offset[1], SIDE - offset[1])

    every = [(y, z, c) for y in range(SIDE) for z in range(SIDE) for c in range(2)]
    order = []
    for offset in sorted(every[1:], key=lambda o: -away(o)):
        for _ in range(4):
            if offset not in order and offset in every[1:]:
                order.append(offset)
            offset = (offset[1], (SIDE - offset[0]) % SIDE, offset[2])
    return order


ORDER = far_first()


def total(value):
    return jnp.sum(jnp.sum(value, axis=0, keepdims=True), axis=1, keepdims=True)


def narrow(value):
    return (value[:, :128] + value[:, 128:256]) + (value[:, 256:384] + value[:, 384:])


def multiply(a, b):
    out = a[:, 0:1] * b[0:1, :]
    for k in range(1, KRYLOV):
        out = out + a[:, k : k + 1] * b[k : k + 1, :]
    return out


def kernel(
    lm_any, rm_any, states_any, state_any, panel_any, left_ref, right_ref,
    out_ref, hess_ref,
    lm_ref, rm_ref, states_ref, state_ref, right_v, turned, spread_l, spread_r, stage_l, stage_r, left_in, right_in, match_v, match_s, panels,
    chosen, grown, joint, left_w, z, x, y, basis, squares, row_ref, last_ref, table, last_table,
    own_sem, send_m, recv_m, send_l, recv_l, send_r, recv_r, send_l2, recv_l2, send_r2, recv_r2,
    send_p, recv_p, send_a, recv_a, send_b, recv_b, send_c, recv_c, send_d, recv_d,
):
    group = lax.axis_index("group")
    me = lax.axis_index("sector")
    groups = lax.axis_size("group")
    n = lax.axis_size("sector")
    near = 2 * SIDE
    line, place = me // near, lax.rem(me, near)
    chip, core = lax.rem(me // 2, SIDE), lax.rem(me, 2)
    channels, block = left_in.shape[0], left_in.shape[1]
    phys = states_ref.shape[1]
    wide = phys * block

    def at(offset):
        dy, dz, dc = offset
        return lax.rem(line + dy, SIDE) * near + lax.rem(chip + dz, SIDE) * 2 + lax.rem(core + dc, 2)

    def back(offset):
        return at((-offset[0] % SIDE, -offset[1] % SIDE, offset[2]))

    def each_peer(body):
        def step(k, _):
            body(lax.rem(me + k, n))
            return 0

        lax.fori_loop(1, n, step, 0)

    barrier = pltpu.get_barrier_semaphore()
    each_peer(lambda peer: pl.semaphore_signal(barrier, inc=1, device_id=(group, peer), device_id_type=MESH))
    for k in range(1, groups):
        for step in range(SIDE):
            other = lax.rem(line + step, SIDE) * near + place
            pl.semaphore_signal(barrier, inc=1, device_id=(lax.rem(group + k, groups), other), device_id_type=MESH)

    loads = [
        pltpu.make_async_copy(src, dst, own_sem.at[i])
        for i, (src, dst) in enumerate(
            (
                (right_ref, right_v),
                (left_ref.at[me], spread_l.at[me]),
                (panel_any, panels.at[group]),
                (lm_any, lm_ref),
                (rm_any, rm_ref),
                (states_any, states_ref),
                (state_any, state_ref),
            )
        )
    ]
    for load in loads:
        load.start()
    for load in loads[:5]:
        load.wait()
    lane = lax.broadcasted_iota(jnp.int32, (1, 128), 1)
    match_v[me] = jnp.where(lane == 0, lm_ref[0], rm_ref[0])
    pl.semaphore_wait(barrier, n - 1 + (groups - 1) * SIDE)

    def remote(src, dst, send, recv, device):
        return pltpu.make_async_remote_copy(
            src_ref=src, dst_ref=dst, send_sem=send, recv_sem=recv, device_id=device, device_id_type=MESH
        )

    def tell(peer, slot):
        return remote(match_v.at[slot], match_v.at[slot], send_m.at[peer], recv_m.at[slot], (group, peer))

    def spread_left(peer, slot):
        return remote(left_ref.at[peer], spread_l.at[slot], send_l.at[peer], recv_l.at[slot], (group, peer))

    def spread_right(peer, slot):
        return remote(turned.at[peer], spread_r.at[slot], send_r.at[peer], recv_r.at[slot], (group, peer))

    def route_left(peer, slot):
        return remote(stage_l.at[peer], left_in.at[slot], send_l2.at[peer], recv_l2.at[slot], (group, peer))

    def route_right(peer, slot):
        return remote(stage_r.at[peer], right_in.at[slot], send_r2.at[peer], recv_r2.at[slot], (group, peer))

    def panel_copy(k, slot):
        other = lax.rem(group + k, groups)
        return remote(panels.at[slot], panels.at[slot], send_p.at[other], recv_p.at[slot], (other, me))

    for offset in ORDER:
        tell(at(offset), me).start()

    def turn(peer):
        turned[peer] = right_v[peer].astype(F32).T.astype(BF16)

    for offset in ORDER:
        peer = at(offset)
        turn(peer)
        spread_right(peer, me).start()
    for k in range(1, groups):
        panel_copy(k, group).start()
    for offset in ORDER:
        spread_left(at(offset), me).start()
    turn(me)
    spread_r[me] = turned[me]

    loads[5].wait()
    loads[6].wait()
    big = jnp.max(jnp.max(jnp.abs(state_ref[...]), axis=0, keepdims=True), axis=1, keepdims=True)
    shrink = jnp.where(big > 0.0, 1.0 / big, 0.0)
    for q in range(phys):
        y[:, q * block : (q + 1) * block] = state_ref[pl.ds(q, block, stride=phys), :] * shrink
    acc = jnp.zeros((8, 128), F32)
    for r in range(0, block, 8):
        piece = y[r : r + 8, :]
        acc = acc + narrow(piece * piece)
    size = jnp.sqrt(total(acc))
    scale = jnp.where(size > 0.0, 1.0 / size, 0.0)
    acc_first = jnp.zeros((8, 128), F32)
    for r in range(0, block, 16):
        first = y[r : r + 16, :] * scale
        basis[0, r : r + 16, :] = first
        x[r : r + 16, :] = first.astype(BF16)
        acc_first = acc_first + narrow(first[:8] * first[:8]) + narrow(first[8:] * first[8:])
    own_square = total(acc_first)
    squares[0:1, :] = jnp.broadcast_to(own_square, (1, 128))
    row_ref[...] = jnp.where(lane == 64, big * size, 0.0)
    last_ref[...] = jnp.zeros((1, 128), F32)

    for k in range(1, groups):
        panel_copy(k, lax.rem(group + k, groups)).wait_recv()
    pick = lax.broadcasted_iota(jnp.int32, (16, 256), 0)
    want = jnp.zeros((16, 256), jnp.int32)
    for p in range(phys):
        for q in range(phys):
            want = jnp.where(pick == p * phys + q, 16 * states_ref[0, q] + states_ref[0, p], want)
    choose = (want == lax.broadcasted_iota(jnp.int32, (16, 256), 1)).astype(BF16)
    chosen[...] = lax.dot_general(
        choose,
        panels[...].reshape(channels * channels, 256),
        (((1,), (1,)), ((), ())),
        preferred_element_type=F32,
    )
    grow = (
        lax.broadcasted_iota(jnp.int32, (channels, 8 * channels), 0)
        == lax.broadcasted_iota(jnp.int32, (channels, 8 * channels), 1) // 8
    ).astype(BF16)
    same = lax.broadcasted_iota(jnp.int32, (1, 8, 8 * channels), 1) == lax.rem(
        lax.broadcasted_iota(jnp.int32, (1, 8, 8 * channels), 2), 8
    )
    for p in range(phys):
        rows = jnp.concatenate(
            [chosen[p * phys : (p + 1) * phys, a * channels : (a + 1) * channels] for a in range(channels)], axis=0
        )
        wider = jnp.dot(rows.astype(BF16), grow, preferred_element_type=F32)
        grown[p] = jnp.where(same, wider[:, None, :], 0.0).reshape(channels * phys * 8, 8 * channels).astype(BF16)

    each_peer(lambda peer: tell(peer, peer).wait_recv())
    to_scalar = pltpu.make_async_copy(match_v, match_s, own_sem.at[7])
    to_scalar.start()
    to_scalar.wait()
    each_peer(lambda peer: spread_right(peer, peer).wait_recv())
    for offset in ORDER:
        peer = at(offset)
        stage_r[peer] = spread_r[match_s[peer, 0, 1]]
        route_right(peer, me).start()
    right_in[me] = spread_r[match_s[me, 0, 1]]

    each_peer(lambda peer: spread_left(peer, peer).wait_recv())
    for offset in ORDER:
        peer = at(offset)
        source = back(offset)
        route_right(source, source).wait_recv()
        stage_l[peer] = spread_l[match_s[peer, 0, 0]]
        route_left(peer, me).start()
    left_in[me] = spread_l[match_s[me, 0, 0]]

    def join(m, _):
        start = pl.multiple_of(m * 16, 16)
        lines_in = right_in[:, pl.ds(start, 16), :].astype(F32)
        both = jnp.concatenate(
            [lines_in[:, :8].reshape(channels * 8, block), lines_in[:, 8:].reshape(channels * 8, block)], axis=1
        ).astype(BF16)
        for p in range(phys):
            out = jnp.dot(grown[p], both, preferred_element_type=F32)
            tiles = out.reshape(channels * phys, 8, 2 * block)
            joint[:, pl.ds(start, 16), p * block : (p + 1) * block] = jnp.concatenate(
                [tiles[:, :, :block], tiles[:, :, block:]], axis=1
            ).astype(BF16)
        return 0

    lax.fori_loop(0, block // 16, join, 0)

    def right_product():
        for a in range(channels):
            weights = joint[a * phys : (a + 1) * phys].reshape(wide, wide)
            z[a] = jnp.dot(x[...], weights, preferred_element_type=F32).astype(BF16)

    def left_product():
        y[...] = jnp.dot(left_w[...], z[...].reshape(channels * block, wide), preferred_element_type=F32)

    right_product()
    each_peer(lambda peer: route_left(peer, peer).wait_recv())
    for a in range(channels):
        left_w[:, a * block : (a + 1) * block] = left_in[a]

    def orthogonalize(t):
        accs = [jnp.zeros((8, 128), F32)] * (t + 1)
        whole = jnp.zeros((8, 128), F32)
        for r in range(0, block, 8):
            piece = y[r : r + 8, :]
            for j in range(t + 1):
                accs[j] = accs[j] + narrow(basis[j, r : r + 8, :] * piece)
            whole = whole + narrow(piece * piece)
        heights = []
        for j in range(t + 1):
            square = squares[j : j + 1, 0:1]
            heights.append(total(accs[j]) * jnp.where(square > 0.0, 1.0 / square, 0.0))
        target = last_ref if t + 1 == KRYLOV else row_ref
        row = target[...]
        for j in range(t + 1):
            row = jnp.where(lane == t * KRYLOV + j, heights[j], row)
        if t + 1 < KRYLOV:
            size = total(whole)
            scale = jnp.where(size > 0.0, lax.rsqrt(size), 0.0)
            acc = jnp.zeros((8, 128), F32)
            for r in range(0, block, 16):
                rest = y[r : r + 16, :]
                for j in range(t + 1):
                    rest = rest - heights[j] * basis[j, r : r + 16, :]
                rest = rest * scale
                basis[t + 1, r : r + 16, :] = rest
                x[r : r + 16, :] = rest.astype(BF16)
                rest = rest * rest
                acc = acc + (narrow(rest[:8]) + narrow(rest[8:]))
            squares[t + 1 : t + 2, :] = jnp.broadcast_to(total(acc), (1, 128))
            row = jnp.where(lane == t * KRYLOV + t + 1, size * scale, row)
        target[...] = row

    def krylov_step(t, _):
        left_product()
        for i in range(KRYLOV - 1):
            pl.when(t == i)(functools.partial(orthogonalize, i))
        pl.when(t + 2 < KRYLOV)(right_product)
        return 0

    lax.fori_loop(0, KRYLOV - 1, krylov_step, 0)

    home = group * SIDE + line
    lines = groups * SIDE

    def near_copy(rows, send, recv, k, slot):
        piece = rows.at[home, pl.ds(slot, 1), :]
        other = line * near + lax.rem(place + k, near)
        return remote(piece, piece, send.at[k], recv.at[slot], (group, other))

    def far_copy(rows, send, recv, k, slot):
        piece = rows.at[slot]
        other = lax.rem(home + k, lines)
        return remote(piece, piece, send.at[k], recv.at[slot], (other // SIDE, lax.rem(other, SIDE) * near + place))

    first_near = functools.partial(near_copy, table, send_a, recv_a)
    first_far = functools.partial(far_copy, table, send_b, recv_b)
    last_near = functools.partial(near_copy, last_table, send_c, recv_c)
    last_far = functools.partial(far_copy, last_table, send_d, recv_d)

    row = row_ref[...]
    for j in range(KRYLOV):
        row = jnp.where(lane == 72 + j, squares[j : j + 1, :], row)
    table[home, pl.ds(place, 1), :] = row
    for k in range(1, near):
        first_near(k, place).start()
    right_product()
    left_product()
    orthogonalize(KRYLOV - 1)
    last_table[home, pl.ds(place, 1), :] = last_ref[...]
    for k in range(1, near):
        last_near(k, place).start()
    for k in range(1, near):
        first_near(k, lax.rem(place + k, near)).wait_recv()
    for k in range(1, lines):
        first_far(k, home).start()
    for k in range(1, near):
        last_near(k, lax.rem(place + k, near)).wait_recv()
    for k in range(1, lines):
        last_far(k, home).start()
    for k in range(1, lines):
        first_far(k, lax.rem(home + k, lines)).wait_recv()

    entries = table[...].reshape(groups * n, 128).T
    columns = [entries[t * KRYLOV : (t + 1) * KRYLOV, :] for t in range(KRYLOV - 1)]
    norms = entries[64:65, :]
    metric = entries[72:80, :]
    sub = lax.broadcasted_iota(jnp.int32, (KRYLOV, 128), 0)
    lanes = lax.broadcasted_iota(jnp.int32, (KRYLOV, 128), 1)
    vectors = [jnp.where(sub == 0, norms / jnp.sqrt(total(norms * norms) + EPS), 0.0)]
    duals = [vectors[0] * metric]
    hess = jnp.zeros((KRYLOV, 128), F32)

    def advance(t, hess):
        now = vectors[t]
        applied = columns[0] * now[0:1, :]
        for i in range(1, t + 1):
            applied = applied + columns[i] * now[i : i + 1, :]
        heights = [total(duals[j] * applied) for j in range(t + 1)]
        for j in range(t + 1):
            hess = jnp.where((sub == j) & (lanes == t), heights[j], hess)
        if t + 1 < KRYLOV:
            rest = applied
            for j in range(t + 1):
                rest = rest - heights[j] * vectors[j]
            beta = jnp.sqrt(total(rest * rest * metric) + EPS)
            hess = jnp.where((sub == t + 1) & (lanes == t), beta, hess)
            vectors.append(rest / beta)
            duals.append(vectors[t + 1] * metric)
        return hess

    for t in range(KRYLOV - 1):
        hess = advance(t, hess)
    for k in range(1, lines):
        last_far(k, lax.rem(home + k, lines)).wait_recv()
    columns.append(last_table[...].reshape(groups * n, 128).T[56:64, :])
    hess = advance(KRYLOV - 1, hess)
    hess_ref[...] = hess[:, :KRYLOV]

    scaled = (-TAU / 16.0) * hess
    unit = jnp.where(sub == lanes, 1.0, 0.0).astype(F32)
    second = multiply(scaled, scaled)
    third = multiply(second, scaled)
    inverse = [1.0 / math.factorial(order) for order in range(11)]
    series = inverse[9] * unit + inverse[10] * scaled
    for order in (6, 3, 0):
        lower = inverse[order] * unit + inverse[order + 1] * scaled + inverse[order + 2] * second
        series = lower + multiply(third, series)
    for _ in range(4):
        series = multiply(series, series)
    coefficients = series[:, 0:1]
    length = float(groups * n * block * wide)
    rescale = jnp.sqrt(jnp.full((1, 1), length, F32)) / jnp.sqrt(
        jnp.sum(coefficients * coefficients, axis=0, keepdims=True)
    )
    mixed = coefficients[0:1, :] * vectors[0]
    for t in range(1, KRYLOV):
        mixed = mixed + coefficients[t : t + 1, :] * vectors[t]
    weight = jnp.sum(jnp.where(lanes == group * n + me, mixed, 0.0), axis=1, keepdims=True) * rescale
    for p in range(phys):
        columns_p = slice(p * block, (p + 1) * block)
        acc = weight[0:1, :] * basis[0, :, columns_p]
        for j in range(1, KRYLOV):
            acc = acc + weight[j : j + 1, :] * basis[j, :, columns_p]
        out_ref[p] = acc

    def finish(peer):
        tell(peer, me).wait_send()
        spread_left(peer, me).wait_send()
        spread_right(peer, me).wait_send()
        route_left(peer, me).wait_send()
        route_right(peer, me).wait_send()

    each_peer(finish)
    for k in range(1, groups):
        panel_copy(k, group).wait_send()
    for k in range(1, near):
        first_near(k, place).wait_send()
        last_near(k, place).wait_send()
    for k in range(1, lines):
        first_far(k, home).wait_send()
        last_far(k, home).wait_send()


def finish_kernel(parts_ref, matrix_ref, state_out, hess_out):
    for p in range(parts_ref.shape[0]):
        state_out[:, p, :] = parts_ref[p]
    hess_out[...] = matrix_ref[...]


def local(state, panel, left_env, right_env, left_match, right_match, phys_states):
    n, groups = lax.axis_size("sector"), lax.axis_size("group")
    channels, block = left_env.shape[1], left_env.shape[2]
    phys = phys_states.shape[1]
    wide = phys * block
    rows = state.reshape(-1, state.shape[-1])
    vmem = pl.BlockSpec(memory_space=pltpu.VMEM)
    whole = pl.BlockSpec(memory_space=pl.ANY)
    piece = (n, block, block)
    dma = pltpu.SemaphoreType.DMA
    parts, matrix = pl.pallas_call(
        kernel,
        out_shape=(
            jax.ShapeDtypeStruct((phys, block, block), F32),
            jax.ShapeDtypeStruct((KRYLOV, KRYLOV), F32),
        ),
        in_specs=[whole] * 7,
        out_specs=(vmem, vmem),
        scratch_shapes=[
            pltpu.SMEM(left_match.shape, jnp.int32),
            pltpu.SMEM(right_match.shape, jnp.int32),
            pltpu.SMEM(phys_states.shape, jnp.int32),
            pltpu.VMEM(rows.shape, F32),
            pltpu.VMEM(piece, BF16),
            pltpu.VMEM(piece, BF16),
            pltpu.VMEM(piece, BF16),
            pltpu.VMEM(piece, BF16),
            pltpu.VMEM(piece, BF16),
            pltpu.VMEM(piece, BF16),
            pltpu.VMEM(piece, BF16),
            pltpu.VMEM(piece, BF16),
            pltpu.VMEM((n, 1, 128), jnp.int32),
            pltpu.SMEM((n, 1, 128), jnp.int32),
            pltpu.VMEM((groups,) + panel.shape, BF16),
            pltpu.VMEM((phys * phys, channels * channels), F32),
            pltpu.VMEM((phys, channels * phys * 8, channels * 8), BF16),
            pltpu.VMEM((channels * phys, block, wide), BF16),
            pltpu.VMEM((block, channels * block), BF16),
            pltpu.VMEM((channels, block, wide), BF16),
            pltpu.VMEM((block, wide), BF16),
            pltpu.VMEM((block, wide), F32),
            pltpu.VMEM((KRYLOV, block, wide), F32),
            pltpu.VMEM((KRYLOV, 128), F32),
            pltpu.VMEM((1, 128), F32),
            pltpu.VMEM((1, 128), F32),
            pltpu.VMEM((groups * SIDE, 2 * SIDE, 128), F32),
            pltpu.VMEM((groups * SIDE, 2 * SIDE, 128), F32),
            dma((8,)),
        ]
        + [dma((n,))] * 10
        + [dma((groups,))] * 2
        + [dma((2 * SIDE,))] * 2
        + [dma((groups * SIDE,))] * 2
        + [dma((2 * SIDE,))] * 2
        + [dma((groups * SIDE,))] * 2,
        compiler_params=pltpu.CompilerParams(collective_id=0, has_side_effects=True, vmem_limit_bytes=VMEM_LIMIT),
        name="step",
    )(left_match, right_match, phys_states, rows, panel, left_env[0], right_env[0])
    new_state, hessenberg = pl.pallas_call(
        finish_kernel,
        out_shape=(
            jax.ShapeDtypeStruct(state.shape[1:], F32),
            jax.ShapeDtypeStruct((KRYLOV, KRYLOV), F32),
        ),
        in_specs=[vmem, vmem],
        out_specs=(vmem, vmem),
        name="finish",
    )(parts, matrix)
    return new_state.reshape(state.shape), hessenberg


def solution(mesh):
    return jax.shard_map(
        local,
        mesh=mesh,
        in_specs=(
            P(("group", "sector"), None, None, None),
            P("group", None, None),
            P(("group", "sector"), None, None, None),
            P(("group", "sector"), None, None, None),
            P(("group", "sector")),
            P(("group", "sector")),
            P(("group", "sector"), None),
        ),
        out_specs=(P(("group", "sector"), None, None, None), P()),
        check_vma=False,
    )
```

```python
import functools
import math

import jax
import jax.numpy as jnp
from jax import lax
from jax.experimental import pallas as pl
from jax.experimental.pallas import tpu as pltpu
from jax.sharding import PartitionSpec as P

MESH = pl.DeviceIdType.MESH
F32 = jnp.float32
BF16 = jnp.bfloat16

KRYLOV = 8
TAU = 3.0
EPS = 1e-06
LEAD = 24
VMEM_LIMIT = 56 * 1024 * 1024
SIDE = 4


def far_first():
    def away(offset):
        return min(offset[0], SIDE - offset[0]) + min(offset[1], SIDE - offset[1])

    every = [(y, z, c) for y in range(SIDE) for z in range(SIDE) for c in range(2)]
    order = []
    for offset in sorted(every[1:], key=lambda o: -away(o)):
        for _ in range(4):
            if offset not in order and offset in every[1:]:
                order.append(offset)
            offset = (offset[1], (SIDE - offset[0]) % SIDE, offset[2])
    return order


ORDER = far_first()
NEAR_STEPS = (4, 5, 3, 2, 6, 1, 7)
FAR_STEPS = (10, 9, 11, 6, 14, 8, 2, 5, 7, 13, 15, 4, 12, 1, 3)


def total(value):
    return jnp.sum(jnp.sum(value, axis=0, keepdims=True), axis=1, keepdims=True)


def narrow(value):
    return (value[:, :128] + value[:, 128:256]) + (value[:, 256:384] + value[:, 384:])


def multiply(a, b):
    out = a[:, 0:1] * b[0:1, :]
    for k in range(1, KRYLOV):
        out = out + a[:, k : k + 1] * b[k : k + 1, :]
    return out


def kernel(
    match_any, states_any, state_any, panel_any, left_ref, right_ref,
    out_ref, hess_ref,
    match_ref, states_ref, state_ref, right_v, turned, spread_l, spread_r, stage_l, stage_r, left_in, right_in, match_v, match_s, panels,
    chosen, grown, joint, left_w, z, x, y, basis, squares, row_ref, last_ref, table, last_table,
    own_sem, send_m, recv_m, send_l, recv_l, send_r, recv_r, send_l2, recv_l2, send_r2, recv_r2,
    send_p, recv_p, send_a, recv_a, send_b, recv_b, send_c, recv_c, send_d, recv_d,
):
    group = lax.axis_index("group")
    me = lax.axis_index("sector")
    groups = lax.axis_size("group")
    n = lax.axis_size("sector")
    near = 2 * SIDE
    line, place = me // near, lax.rem(me, near)
    chip, core = lax.rem(me // 2, SIDE), lax.rem(me, 2)
    channels, block = left_in.shape[0], left_in.shape[1]
    phys = states_ref.shape[1]
    wide = phys * block

    def at(offset):
        dy, dz, dc = offset
        return lax.rem(line + dy, SIDE) * near + lax.rem(chip + dz, SIDE) * 2 + lax.rem(core + dc, 2)

    def back(offset):
        return at((-offset[0] % SIDE, -offset[1] % SIDE, offset[2]))

    def each_peer(body):
        def step(k, _):
            body(lax.rem(me + k, n))
            return 0

        lax.fori_loop(1, n, step, 0)

    barrier = pltpu.get_barrier_semaphore()
    each_peer(lambda peer: pl.semaphore_signal(barrier, inc=1, device_id=(group, peer), device_id_type=MESH))
    for k in range(1, groups):
        for step in range(SIDE):
            other = lax.rem(line + step, SIDE) * near + place
            pl.semaphore_signal(barrier, inc=1, device_id=(lax.rem(group + k, groups), other), device_id_type=MESH)

    loads = [
        pltpu.make_async_copy(src, dst, own_sem.at[i])
        for i, (src, dst) in enumerate(
            (
                (right_ref, right_v),
                (left_ref.at[me], spread_l.at[me]),
                (panel_any, panels.at[group]),
                (match_any, match_ref),
                (states_any, states_ref),
                (state_any, state_ref),
            )
        )
    ]
    for load in loads:
        load.start()
    for load in loads[:4]:
        load.wait()
    lane = lax.broadcasted_iota(jnp.int32, (1, 128), 1)
    match_v[me] = jnp.where(lane == 0, match_ref[0, 0] // n, lax.rem(match_ref[0, 0], n))
    pl.semaphore_wait(barrier, n - 1 + (groups - 1) * SIDE)

    def remote(src, dst, send, recv, device):
        return pltpu.make_async_remote_copy(
            src_ref=src, dst_ref=dst, send_sem=send, recv_sem=recv, device_id=device, device_id_type=MESH
        )

    def tell(peer, slot):
        return remote(match_v.at[slot], match_v.at[slot], send_m.at[peer], recv_m.at[slot], (group, peer))

    def spread_left(peer, slot):
        return remote(left_ref.at[peer], spread_l.at[slot], send_l.at[peer], recv_l.at[slot], (group, peer))

    def spread_right(peer, slot):
        return remote(turned.at[peer], spread_r.at[slot], send_r.at[peer], recv_r.at[slot], (group, peer))

    def route_left(peer, slot):
        return remote(stage_l.at[peer], left_in.at[slot], send_l2.at[peer], recv_l2.at[slot], (group, peer))

    def route_right(peer, slot):
        return remote(stage_r.at[peer], right_in.at[slot], send_r2.at[peer], recv_r2.at[slot], (group, peer))

    def panel_copy(k, slot):
        other = lax.rem(group + k, groups)
        return remote(panels.at[slot], panels.at[slot], send_p.at[other], recv_p.at[slot], (other, me))

    for offset in ORDER:
        tell(at(offset), me).start()

    def turn(peer):
        turned[peer] = right_v[peer].astype(F32).T.astype(BF16)

    for offset in ORDER:
        peer = at(offset)
        turn(peer)
        spread_right(peer, me).start()
    for k in range(1, groups):
        panel_copy(k, group).start()
    for i, offset in enumerate(ORDER):
        source = back(offset)
        spread_right(source, source).wait_recv()
        spread_left(at(offset), me).start()
    turn(me)
    spread_r[me] = turned[me]

    loads[4].wait()
    loads[5].wait()
    big = jnp.max(jnp.max(jnp.abs(state_ref[...]), axis=0, keepdims=True), axis=1, keepdims=True)
    shrink = jnp.where(big > 0.0, 1.0 / big, 0.0)
    for q in range(phys):
        y[:, q * block : (q + 1) * block] = state_ref[pl.ds(q, block, stride=phys), :] * shrink
    acc = jnp.zeros((8, 128), F32)
    for r in range(0, block, 8):
        piece = y[r : r + 8, :]
        acc = acc + narrow(piece * piece)
    size = jnp.sqrt(total(acc))
    scale = jnp.where(size > 0.0, 1.0 / size, 0.0)
    acc_first = jnp.zeros((8, 128), F32)
    for r in range(0, block, 16):
        first = y[r : r + 16, :] * scale
        basis[0, r : r + 16, :] = first
        x[r : r + 16, :] = first.astype(BF16)
        acc_first = acc_first + narrow(first[:8] * first[:8]) + narrow(first[8:] * first[8:])
    own_square = total(acc_first)
    squares[0:1, :] = jnp.broadcast_to(own_square, (1, 128))
    row_ref[...] = jnp.where(lane == 64, big * size, 0.0)
    last_ref[...] = jnp.zeros((1, 128), F32)

    for k in range(1, groups):
        panel_copy(k, lax.rem(group + k, groups)).wait_recv()
    pick = lax.broadcasted_iota(jnp.int32, (16, 256), 0)
    want = jnp.zeros((16, 256), jnp.int32)
    for p in range(phys):
        for q in range(phys):
            want = jnp.where(pick == p * phys + q, 16 * states_ref[0, q] + states_ref[0, p], want)
    choose = (want == lax.broadcasted_iota(jnp.int32, (16, 256), 1)).astype(BF16)
    chosen[...] = lax.dot_general(
        choose,
        panels[...].reshape(channels * channels, 256),
        (((1,), (1,)), ((), ())),
        preferred_element_type=F32,
    )
    grow = (
        lax.broadcasted_iota(jnp.int32, (channels, 8 * channels), 0)
        == lax.broadcasted_iota(jnp.int32, (channels, 8 * channels), 1) // 8
    ).astype(BF16)
    same = lax.broadcasted_iota(jnp.int32, (1, 8, 8 * channels), 1) == lax.rem(
        lax.broadcasted_iota(jnp.int32, (1, 8, 8 * channels), 2), 8
    )
    for p in range(phys):
        rows = jnp.concatenate(
            [chosen[p * phys : (p + 1) * phys, a * channels : (a + 1) * channels] for a in range(channels)], axis=0
        )
        wider = jnp.dot(rows.astype(BF16), grow, preferred_element_type=F32)
        grown[p] = jnp.where(same, wider[:, None, :], 0.0).reshape(channels * phys * 8, 8 * channels).astype(BF16)

    each_peer(lambda peer: tell(peer, peer).wait_recv())
    to_scalar = pltpu.make_async_copy(match_v, match_s, own_sem.at[7])
    to_scalar.start()
    to_scalar.wait()
    for offset in ORDER:
        peer = at(offset)
        stage_r[peer] = spread_r[match_s[peer, 0, 1]]
        route_right(peer, me).start()
    right_in[me] = spread_r[match_s[me, 0, 1]]

    each_peer(lambda peer: spread_left(peer, peer).wait_recv())
    here = 0
    for i, offset in enumerate(ORDER):
        peer = at(offset)
        while here < min(i + LEAD, len(ORDER)):
            source = back(ORDER[here])
            route_right(source, source).wait_recv()
            here += 1
        stage_l[peer] = spread_l[match_s[peer, 0, 0]]
        route_left(peer, me).start()
    left_in[me] = spread_l[match_s[me, 0, 0]]

    def join(m, _):
        start = pl.multiple_of(m * 16, 16)
        lines_in = right_in[:, pl.ds(start, 16), :].astype(F32)
        both = jnp.concatenate(
            [lines_in[:, :8].reshape(channels * 8, block), lines_in[:, 8:].reshape(channels * 8, block)], axis=1
        ).astype(BF16)
        for p in range(phys):
            out = jnp.dot(grown[p], both, preferred_element_type=F32)
            tiles = out.reshape(channels * phys, 8, 2 * block)
            joint[:, pl.ds(start, 16), p * block : (p + 1) * block] = jnp.concatenate(
                [tiles[:, :, :block], tiles[:, :, block:]], axis=1
            ).astype(BF16)
        return 0

    lax.fori_loop(0, block // 16, join, 0)

    def right_product():
        for a in range(channels):
            weights = joint[a * phys : (a + 1) * phys].reshape(wide, wide)
            z[a] = jnp.dot(x[...], weights, preferred_element_type=F32).astype(BF16)

    def left_product():
        y[...] = jnp.dot(left_w[...], z[...].reshape(channels * block, wide), preferred_element_type=F32)

    right_product()

    sources = [me] + [back(offset) for offset in ORDER]
    for start in range(0, n, 8):
        batch = sources[start : start + 8]
        for source in batch:
            if source is not me:
                route_left(source, source).wait_recv()
            left_w[:, pl.ds(pl.multiple_of(source * block, block), block)] = left_in[source]
        out = jnp.dot(
            jnp.concatenate([left_in[source] for source in batch], axis=1),
            jnp.concatenate([z[source] for source in batch], axis=0),
            preferred_element_type=F32,
        )
        y[...] = out if start == 0 else y[...] + out

    def orthogonalize(t):
        accs = [jnp.zeros((8, 128), F32)] * (t + 1)
        whole = jnp.zeros((8, 128), F32)
        for r in range(0, block, 8):
            piece = y[r : r + 8, :]
            for j in range(t + 1):
                accs[j] = accs[j] + narrow(basis[j, r : r + 8, :] * piece)
            whole = whole + narrow(piece * piece)
        heights = []
        for j in range(t + 1):
            square = squares[j : j + 1, 0:1]
            heights.append(total(accs[j]) * jnp.where(square > 0.0, 1.0 / square, 0.0))
        target = last_ref if t + 1 == KRYLOV else row_ref
        row = target[...]
        for j in range(t + 1):
            row = jnp.where(lane == t * KRYLOV + j, heights[j], row)
        if t + 1 < KRYLOV:
            size = total(whole)
            scale = jnp.where(size > 0.0, lax.rsqrt(size), 0.0)
            acc = jnp.zeros((8, 128), F32)
            for r in range(0, block, 16):
                rest = y[r : r + 16, :]
                for j in range(t + 1):
                    rest = rest - heights[j] * basis[j, r : r + 16, :]
                rest = rest * scale
                basis[t + 1, r : r + 16, :] = rest
                x[r : r + 16, :] = rest.astype(BF16)
                rest = rest * rest
                acc = acc + (narrow(rest[:8]) + narrow(rest[8:]))
            squares[t + 1 : t + 2, :] = jnp.broadcast_to(total(acc), (1, 128))
            row = jnp.where(lane == t * KRYLOV + t + 1, size * scale, row)
        target[...] = row

    def krylov_step(t, _):
        for i in range(KRYLOV - 1):
            pl.when(t == i)(functools.partial(orthogonalize, i))

        @pl.when(t + 2 < KRYLOV)
        def _():
            right_product()
            left_product()

        return 0

    lax.fori_loop(0, KRYLOV - 1, krylov_step, 0)

    home = group * SIDE + line
    lines = groups * SIDE

    def near_copy(rows, send, recv, k, slot):
        piece = rows.at[home, pl.ds(slot, 1), :]
        other = line * near + lax.rem(place + k, near)
        return remote(piece, piece, send.at[k], recv.at[slot], (group, other))

    def far_copy(rows, send, recv, k, slot):
        piece = rows.at[slot]
        other = lax.rem(home + k, lines)
        return remote(piece, piece, send.at[k], recv.at[slot], (other // SIDE, lax.rem(other, SIDE) * near + place))

    first_near = functools.partial(near_copy, table, send_a, recv_a)
    first_far = functools.partial(far_copy, table, send_b, recv_b)
    last_near = functools.partial(near_copy, last_table, send_c, recv_c)
    last_far = functools.partial(far_copy, last_table, send_d, recv_d)

    row = row_ref[...]
    for j in range(KRYLOV):
        row = jnp.where(lane == 72 + j, squares[j : j + 1, :], row)
    table[home, pl.ds(place, 1), :] = row
    for k in NEAR_STEPS:
        first_near(k, place).start()
    right_product()
    left_product()
    orthogonalize(KRYLOV - 1)
    last_table[home, pl.ds(place, 1), :] = last_ref[...]
    for k in NEAR_STEPS:
        last_near(k, place).start()
    for k in range(1, near):
        first_near(k, lax.rem(place + k, near)).wait_recv()
    for k in FAR_STEPS:
        first_far(k, home).start()
    for k in range(1, near):
        last_near(k, lax.rem(place + k, near)).wait_recv()
    for k in FAR_STEPS:
        last_far(k, home).start()
    for k in range(1, lines):
        first_far(k, lax.rem(home + k, lines)).wait_recv()

    entries = table[...].reshape(groups * n, 128).T
    columns = [entries[t * KRYLOV : (t + 1) * KRYLOV, :] for t in range(KRYLOV - 1)]
    norms = entries[64:65, :]
    metric = entries[72:80, :]
    sub = lax.broadcasted_iota(jnp.int32, (KRYLOV, 128), 0)
    lanes = lax.broadcasted_iota(jnp.int32, (KRYLOV, 128), 1)
    vectors = [jnp.where(sub == 0, norms / jnp.sqrt(total(norms * norms) + EPS), 0.0)]
    duals = [vectors[0] * metric]
    hess = jnp.zeros((KRYLOV, 128), F32)

    def advance(t, hess):
        now = vectors[t]
        applied = columns[0] * now[0:1, :]
        for i in range(1, t + 1):
            applied = applied + columns[i] * now[i : i + 1, :]
        heights = [total(duals[j] * applied) for j in range(t + 1)]
        for j in range(t + 1):
            hess = jnp.where((sub == j) & (lanes == t), heights[j], hess)
        if t + 1 < KRYLOV:
            rest = applied
            for j in range(t + 1):
                rest = rest - heights[j] * vectors[j]
            beta = jnp.sqrt(total(rest * rest * metric) + EPS)
            hess = jnp.where((sub == t + 1) & (lanes == t), beta, hess)
            vectors.append(rest / beta)
            duals.append(vectors[t + 1] * metric)
        return hess

    for t in range(KRYLOV - 1):
        hess = advance(t, hess)
    for k in range(1, lines):
        last_far(k, lax.rem(home + k, lines)).wait_recv()
    columns.append(last_table[...].reshape(groups * n, 128).T[56:64, :])
    hess = advance(KRYLOV - 1, hess)
    hess_ref[...] = hess[:, :KRYLOV]

    scaled = (-TAU / 16.0) * hess
    unit = jnp.where(sub == lanes, 1.0, 0.0).astype(F32)
    second = multiply(scaled, scaled)
    third = multiply(second, scaled)
    inverse = [1.0 / math.factorial(order) for order in range(11)]
    series = inverse[9] * unit + inverse[10] * scaled
    for order in (6, 3, 0):
        lower = inverse[order] * unit + inverse[order + 1] * scaled + inverse[order + 2] * second
        series = lower + multiply(third, series)
    for _ in range(4):
        series = multiply(series, series)
    coefficients = series[:, 0:1]
    length = float(groups * n * block * wide)
    rescale = jnp.sqrt(jnp.full((1, 1), length, F32)) / jnp.sqrt(
        jnp.sum(coefficients * coefficients, axis=0, keepdims=True)
    )
    mixed = coefficients[0:1, :] * vectors[0]
    for t in range(1, KRYLOV):
        mixed = mixed + coefficients[t : t + 1, :] * vectors[t]
    weight = jnp.sum(jnp.where(lanes == group * n + me, mixed, 0.0), axis=1, keepdims=True) * rescale
    for p in range(phys):
        columns_p = slice(p * block, (p + 1) * block)
        acc = weight[0:1, :] * basis[0, :, columns_p]
        for j in range(1, KRYLOV):
            acc = acc + weight[j : j + 1, :] * basis[j, :, columns_p]
        out_ref[:, p, :] = acc

    def finish(peer):
        tell(peer, me).wait_send()
        spread_left(peer, me).wait_send()
        spread_right(peer, me).wait_send()
        route_left(peer, me).wait_send()
        route_right(peer, me).wait_send()

    each_peer(finish)
    for k in range(1, groups):
        panel_copy(k, group).wait_send()
    for k in range(1, near):
        first_near(k, place).wait_send()
        last_near(k, place).wait_send()
    for k in range(1, lines):
        first_far(k, home).wait_send()
        last_far(k, home).wait_send()


def finish_kernel(state_in, matrix_in, state_out, matrix_out, sems):
    copies = [
        pltpu.make_async_copy(state_in, state_out, sems.at[0]),
        pltpu.make_async_copy(matrix_in, matrix_out, sems.at[1]),
    ]
    for copy in copies:
        copy.start()
    for copy in copies:
        copy.wait()


def local(state, panel, left_env, right_env, left_match, right_match, phys_states):
    n, groups = lax.axis_size("sector"), lax.axis_size("group")
    channels, block = left_env.shape[1], left_env.shape[2]
    phys = phys_states.shape[1]
    wide = phys * block
    rows = state.reshape(-1, state.shape[-1])
    vmem = pl.BlockSpec(memory_space=pltpu.VMEM)
    whole = pl.BlockSpec(memory_space=pl.ANY)
    piece = (n, block, block)
    matches = (left_match * n + right_match).reshape(1, 1)
    dma = pltpu.SemaphoreType.DMA
    parts, matrix = pl.pallas_call(
        kernel,
        out_shape=(
            jax.ShapeDtypeStruct(state.shape[1:], F32),
            jax.ShapeDtypeStruct((KRYLOV, KRYLOV), F32),
        ),
        in_specs=[whole] * 6,
        out_specs=(vmem, vmem),
        scratch_shapes=[
            pltpu.SMEM((1, 1), jnp.int32),
            pltpu.SMEM(phys_states.shape, jnp.int32),
            pltpu.VMEM(rows.shape, F32),
            pltpu.VMEM(piece, BF16),
            pltpu.VMEM(piece, BF16),
            pltpu.VMEM(piece, BF16),
            pltpu.VMEM(piece, BF16),
            pltpu.VMEM(piece, BF16),
            pltpu.VMEM(piece, BF16),
            pltpu.VMEM(piece, BF16),
            pltpu.VMEM(piece, BF16),
            pltpu.VMEM((n, 1, 128), jnp.int32),
            pltpu.SMEM((n, 1, 128), jnp.int32),
            pltpu.VMEM((groups,) + panel.shape, BF16),
            pltpu.VMEM((phys * phys, channels * channels), F32),
            pltpu.VMEM((phys, channels * phys * 8, channels * 8), BF16),
            pltpu.VMEM((channels * phys, block, wide), BF16),
            pltpu.VMEM((block, channels * block), BF16),
            pltpu.VMEM((channels, block, wide), BF16),
            pltpu.VMEM((block, wide), BF16),
            pltpu.VMEM((block, wide), F32),
            pltpu.VMEM((KRYLOV, block, wide), F32),
            pltpu.VMEM((KRYLOV, 128), F32),
            pltpu.VMEM((1, 128), F32),
            pltpu.VMEM((1, 128), F32),
            pltpu.VMEM((groups * SIDE, 2 * SIDE, 128), F32),
            pltpu.VMEM((groups * SIDE, 2 * SIDE, 128), F32),
            dma((8,)),
        ]
        + [dma((n,))] * 10
        + [dma((groups,))] * 2
        + [dma((2 * SIDE,))] * 2
        + [dma((groups * SIDE,))] * 2
        + [dma((2 * SIDE,))] * 2
        + [dma((groups * SIDE,))] * 2,
        compiler_params=pltpu.CompilerParams(collective_id=0, has_side_effects=True, vmem_limit_bytes=VMEM_LIMIT),
        name="step",
    )(matches, phys_states, rows, panel, left_env[0], right_env[0])
    new_state, hessenberg = pl.pallas_call(
        finish_kernel,
        out_shape=(
            jax.ShapeDtypeStruct(state.shape[1:], F32),
            jax.ShapeDtypeStruct((KRYLOV, KRYLOV), F32),
        ),
        in_specs=[vmem, vmem],
        out_specs=(whole, whole),
        scratch_shapes=[dma((2,))],
        name="finish",
    )(parts, matrix)
    return new_state.reshape(state.shape), hessenberg


def solution(mesh):
    return jax.shard_map(
        local,
        mesh=mesh,
        in_specs=(
            P(("group", "sector"), None, None, None),
            P("group", None, None),
            P(("group", "sector"), None, None, None),
            P(("group", "sector"), None, None, None),
            P(("group", "sector")),
            P(("group", "sector")),
            P(("group", "sector"), None),
        ),
        out_specs=(P(("group", "sector"), None, None, None), P()),
        check_vma=False,
    )
```

```python
import functools
import math

import jax
import jax.numpy as jnp
from jax import lax
from jax.experimental import pallas as pl
from jax.experimental.pallas import tpu as pltpu
from jax.sharding import PartitionSpec as P

MESH = pl.DeviceIdType.MESH
F32 = jnp.float32
BF16 = jnp.bfloat16

KRYLOV = 8
TAU = 3.0
EPS = 1e-06
LEAD = 24
VMEM_LIMIT = 56 * 1024 * 1024
SIDE = 4


def far_first():
    def away(offset):
        return min(offset[0], SIDE - offset[0]) + min(offset[1], SIDE - offset[1])

    every = [(y, z, c) for y in range(SIDE) for z in range(SIDE) for c in range(2)]
    order = []
    for offset in sorted(every[1:], key=lambda o: -away(o)):
        for _ in range(4):
            if offset not in order and offset in every[1:]:
                order.append(offset)
            offset = (offset[1], (SIDE - offset[0]) % SIDE, offset[2])
    return order


ORDER = far_first()
NEAR_STEPS = (4, 5, 3, 2, 6, 1, 7)
FAR_STEPS = (10, 9, 11, 6, 14, 8, 2, 5, 7, 13, 15, 4, 12, 1, 3)


def total(value):
    return jnp.sum(jnp.sum(value, axis=0, keepdims=True), axis=1, keepdims=True)


def narrow(value):
    return (value[:, :128] + value[:, 128:256]) + (value[:, 256:384] + value[:, 384:])


def multiply(a, b):
    out = a[:, 0:1] * b[0:1, :]
    for k in range(1, KRYLOV):
        out = out + a[:, k : k + 1] * b[k : k + 1, :]
    return out


def kernel(
    match_any, states_any, state_any, panel_any, left_ref, right_ref,
    out_ref, hess_ref,
    match_ref, states_ref, state_ref, right_v, turned, spread_l, spread_r, stage_l, stage_r, left_in, right_in, match_v, match_s, panels,
    chosen, grown, joint, left_w, z, x, y, basis, squares, row_ref, last_ref, table, last_table,
    own_sem, send_m, recv_m, send_l, recv_l, send_r, recv_r, send_l2, recv_l2, send_r2, recv_r2,
    send_p, recv_p, send_a, recv_a, send_b, recv_b, send_c, recv_c, send_d, recv_d,
):
    group = lax.axis_index("group")
    me = lax.axis_index("sector")
    groups = lax.axis_size("group")
    n = lax.axis_size("sector")
    near = 2 * SIDE
    line, place = me // near, lax.rem(me, near)
    chip, core = lax.rem(me // 2, SIDE), lax.rem(me, 2)
    channels, block = left_in.shape[0], left_in.shape[1]
    phys = states_ref.shape[1]
    wide = phys * block

    def at(offset):
        dy, dz, dc = offset
        return lax.rem(line + dy, SIDE) * near + lax.rem(chip + dz, SIDE) * 2 + lax.rem(core + dc, 2)

    def back(offset):
        return at((-offset[0] % SIDE, -offset[1] % SIDE, offset[2]))

    def each_peer(body):
        def step(k, _):
            body(lax.rem(me + k, n))
            return 0

        lax.fori_loop(1, n, step, 0)

    barrier = pltpu.get_barrier_semaphore()
    each_peer(lambda peer: pl.semaphore_signal(barrier, inc=1, device_id=(group, peer), device_id_type=MESH))
    for k in range(1, groups):
        for step in range(SIDE):
            other = lax.rem(line + step, SIDE) * near + place
            pl.semaphore_signal(barrier, inc=1, device_id=(lax.rem(group + k, groups), other), device_id_type=MESH)

    loads = [
        pltpu.make_async_copy(src, dst, own_sem.at[i])
        for i, (src, dst) in enumerate(
            (
                (right_ref, right_v),
                (left_ref.at[me], spread_l.at[me]),
                (panel_any, panels.at[group]),
                (match_any, match_ref),
                (states_any, states_ref),
                (state_any, state_ref),
            )
        )
    ]
    for load in loads:
        load.start()
    for load in loads[:4]:
        load.wait()
    lane = lax.broadcasted_iota(jnp.int32, (1, 128), 1)
    match_v[me] = jnp.where(lane == 0, match_ref[0, 0] // n, lax.rem(match_ref[0, 0], n))
    pl.semaphore_wait(barrier, n - 1 + (groups - 1) * SIDE)

    def remote(src, dst, send, recv, device):
        return pltpu.make_async_remote_copy(
            src_ref=src, dst_ref=dst, send_sem=send, recv_sem=recv, device_id=device, device_id_type=MESH
        )

    def tell(peer, slot):
        return remote(match_v.at[slot], match_v.at[slot], send_m.at[peer], recv_m.at[slot], (group, peer))

    def spread_left(peer, slot):
        return remote(left_ref.at[peer], spread_l.at[slot], send_l.at[peer], recv_l.at[slot], (group, peer))

    def spread_right(peer, slot):
        return remote(turned.at[peer], spread_r.at[slot], send_r.at[peer], recv_r.at[slot], (group, peer))

    def route_left(peer, slot):
        return remote(stage_l.at[peer], left_in.at[slot], send_l2.at[peer], recv_l2.at[slot], (group, peer))

    def route_right(peer, slot):
        return remote(stage_r.at[peer], right_in.at[slot], send_r2.at[peer], recv_r2.at[slot], (group, peer))

    def panel_copy(k, slot):
        other = lax.rem(group + k, groups)
        return remote(panels.at[slot], panels.at[slot], send_p.at[other], recv_p.at[slot], (other, me))

    for offset in ORDER:
        tell(at(offset), me).start()

    def turn(peer):
        turned[peer] = right_v[peer].astype(F32).T.astype(BF16)

    for offset in ORDER:
        peer = at(offset)
        turn(peer)
        spread_right(peer, me).start()
    for k in range(1, groups):
        panel_copy(k, group).start()
    for i, offset in enumerate(ORDER):
        source = back(offset)
        spread_right(source, source).wait_recv()
        spread_left(at(offset), me).start()
    turn(me)
    spread_r[me] = turned[me]

    loads[4].wait()
    loads[5].wait()
    big = jnp.max(jnp.max(jnp.abs(state_ref[...]), axis=0, keepdims=True), axis=1, keepdims=True)
    shrink = jnp.where(big > 0.0, 1.0 / big, 0.0)
    for q in range(phys):
        y[:, q * block : (q + 1) * block] = state_ref[pl.ds(q, block, stride=phys), :] * shrink
    acc = jnp.zeros((8, 128), F32)
    for r in range(0, block, 8):
        piece = y[r : r + 8, :]
        acc = acc + narrow(piece * piece)
    size = jnp.sqrt(total(acc))
    scale = jnp.where(size > 0.0, 1.0 / size, 0.0)
    acc_first = jnp.zeros((8, 128), F32)
    for r in range(0, block, 16):
        first = y[r : r + 16, :] * scale
        basis[0, r : r + 16, :] = first
        x[r : r + 16, :] = first.astype(BF16)
        acc_first = acc_first + narrow(first[:8] * first[:8]) + narrow(first[8:] * first[8:])
    own_square = total(acc_first)
    squares[0:1, :] = jnp.broadcast_to(own_square, (1, 128))
    row_ref[...] = jnp.where(lane == 64, big * size, 0.0)
    last_ref[...] = jnp.zeros((1, 128), F32)

    for k in range(1, groups):
        panel_copy(k, lax.rem(group + k, groups)).wait_recv()
    pick = lax.broadcasted_iota(jnp.int32, (16, 256), 0)
    want = jnp.zeros((16, 256), jnp.int32)
    for p in range(phys):
        for q in range(phys):
            want = jnp.where(pick == p * phys + q, 16 * states_ref[0, q] + states_ref[0, p], want)
    choose = (want == lax.broadcasted_iota(jnp.int32, (16, 256), 1)).astype(BF16)
    chosen[...] = lax.dot_general(
        choose,
        panels[...].reshape(channels * channels, 256),
        (((1,), (1,)), ((), ())),
        preferred_element_type=F32,
    )
    grow = (
        lax.broadcasted_iota(jnp.int32, (channels, 8 * channels), 0)
        == lax.broadcasted_iota(jnp.int32, (channels, 8 * channels), 1) // 8
    ).astype(BF16)
    same = lax.broadcasted_iota(jnp.int32, (1, 8, 8 * channels), 1) == lax.rem(
        lax.broadcasted_iota(jnp.int32, (1, 8, 8 * channels), 2), 8
    )
    for p in range(phys):
        rows = jnp.concatenate(
            [chosen[p * phys : (p + 1) * phys, a * channels : (a + 1) * channels] for a in range(channels)], axis=0
        )
        wider = jnp.dot(rows.astype(BF16), grow, preferred_element_type=F32)
        grown[p] = jnp.where(same, wider[:, None, :], 0.0).reshape(channels * phys * 8, 8 * channels).astype(BF16)

    each_peer(lambda peer: tell(peer, peer).wait_recv())
    to_scalar = pltpu.make_async_copy(match_v, match_s, own_sem.at[7])
    to_scalar.start()
    to_scalar.wait()
    for offset in ORDER:
        peer = at(offset)
        stage_r[peer] = spread_r[match_s[peer, 0, 1]]
        route_right(peer, me).start()
    right_in[me] = spread_r[match_s[me, 0, 1]]

    each_peer(lambda peer: spread_left(peer, peer).wait_recv())
    here = 0
    for i, offset in enumerate(ORDER):
        peer = at(offset)
        while here < min(i + LEAD, len(ORDER)):
            source = back(ORDER[here])
            route_right(source, source).wait_recv()
            here += 1
        stage_l[peer] = spread_l[match_s[peer, 0, 0]]
        route_left(peer, me).start()
    left_in[me] = spread_l[match_s[me, 0, 0]]

    def join(m, _):
        start = pl.multiple_of(m * 16, 16)
        lines_in = right_in[:, pl.ds(start, 16), :].astype(F32)
        both = jnp.concatenate(
            [lines_in[:, :8].reshape(channels * 8, block), lines_in[:, 8:].reshape(channels * 8, block)], axis=1
        ).astype(BF16)
        for p in range(phys):
            out = jnp.dot(grown[p], both, preferred_element_type=F32)
            tiles = out.reshape(channels * phys, 8, 2 * block)
            joint[:, pl.ds(start, 16), p * block : (p + 1) * block] = jnp.concatenate(
                [tiles[:, :, :block], tiles[:, :, block:]], axis=1
            ).astype(BF16)
        return 0

    lax.fori_loop(0, block // 16, join, 0)

    def right_product():
        for a in range(channels):
            weights = joint[a * phys : (a + 1) * phys].reshape(wide, wide)
            z[a] = jnp.dot(x[...], weights, preferred_element_type=F32).astype(BF16)

    def left_product():
        y[...] = jnp.dot(left_w[...], z[...].reshape(channels * block, wide), preferred_element_type=F32)

    right_product()

    sources = [me] + [back(offset) for offset in ORDER]
    for start in range(0, n, 8):
        batch = sources[start : start + 8]
        for source in batch:
            if source is not me:
                route_left(source, source).wait_recv()
            left_w[:, pl.ds(pl.multiple_of(source * block, block), block)] = left_in[source]
        out = jnp.dot(
            jnp.concatenate([left_in[source] for source in batch], axis=1),
            jnp.concatenate([z[source] for source in batch], axis=0),
            preferred_element_type=F32,
        )
        y[...] = out if start == 0 else y[...] + out

    def orthogonalize(t):
        accs = [jnp.zeros((8, 128), F32)] * (t + 1)
        whole = jnp.zeros((8, 128), F32)
        for r in range(0, block, 8):
            piece = y[r : r + 8, :]
            for j in range(t + 1):
                accs[j] = accs[j] + narrow(basis[j, r : r + 8, :] * piece)
            whole = whole + narrow(piece * piece)
        heights = []
        for j in range(t + 1):
            square = squares[j : j + 1, 0:1]
            heights.append(total(accs[j]) * jnp.where(square > 0.0, 1.0 / square, 0.0))
        target = last_ref if t + 1 == KRYLOV else row_ref
        row = target[...]
        for j in range(t + 1):
            row = jnp.where(lane == t * KRYLOV + j, heights[j], row)
        if t + 1 < KRYLOV:
            size = total(whole)
            scale = jnp.where(size > 0.0, lax.rsqrt(size), 0.0)
            acc = jnp.zeros((8, 128), F32)
            for r in range(0, block, 16):
                rest = y[r : r + 16, :]
                for j in range(t + 1):
                    rest = rest - heights[j] * basis[j, r : r + 16, :]
                rest = rest * scale
                basis[t + 1, r : r + 16, :] = rest
                x[r : r + 16, :] = rest.astype(BF16)
                rest = rest * rest
                acc = acc + (narrow(rest[:8]) + narrow(rest[8:]))
            squares[t + 1 : t + 2, :] = jnp.broadcast_to(total(acc), (1, 128))
            row = jnp.where(lane == t * KRYLOV + t + 1, size * scale, row)
        target[...] = row

    def krylov_step(t, _):
        for i in range(KRYLOV - 1):
            pl.when(t == i)(functools.partial(orthogonalize, i))

        @pl.when(t + 2 < KRYLOV)
        def _():
            right_product()
            left_product()

        return 0

    lax.fori_loop(0, KRYLOV - 1, krylov_step, 0)

    home = group * SIDE + line
    lines = groups * SIDE

    def near_copy(rows, send, recv, k, slot):
        piece = rows.at[home, pl.ds(slot, 1), :]
        other = line * near + lax.rem(place + k, near)
        return remote(piece, piece, send.at[k], recv.at[slot], (group, other))

    def far_copy(rows, send, recv, k, slot):
        piece = rows.at[slot]
        other = lax.rem(home + k, lines)
        return remote(piece, piece, send.at[k], recv.at[slot], (other // SIDE, lax.rem(other, SIDE) * near + place))

    first_near = functools.partial(near_copy, table, send_a, recv_a)
    first_far = functools.partial(far_copy, table, send_b, recv_b)
    last_near = functools.partial(near_copy, last_table, send_c, recv_c)
    last_far = functools.partial(far_copy, last_table, send_d, recv_d)

    row = row_ref[...]
    for j in range(KRYLOV):
        row = jnp.where(lane == 72 + j, squares[j : j + 1, :], row)
    table[home, pl.ds(place, 1), :] = row
    for k in NEAR_STEPS:
        first_near(k, place).start()
    right_product()
    left_product()
    orthogonalize(KRYLOV - 1)
    last_table[home, pl.ds(place, 1), :] = last_ref[...]
    for k in NEAR_STEPS:
        last_near(k, place).start()
    for k in range(1, near):
        first_near(k, lax.rem(place + k, near)).wait_recv()
    for k in FAR_STEPS:
        first_far(k, home).start()

    def left_here(peer):
        tell(peer, me).wait_send()
        spread_left(peer, me).wait_send()
        spread_right(peer, me).wait_send()
        route_left(peer, me).wait_send()
        route_right(peer, me).wait_send()

    each_peer(left_here)
    for k in range(1, groups):
        panel_copy(k, group).wait_send()
    for k in range(1, near):
        last_near(k, lax.rem(place + k, near)).wait_recv()
    for k in FAR_STEPS:
        last_far(k, home).start()
    for k in range(1, lines):
        first_far(k, lax.rem(home + k, lines)).wait_recv()

    entries = table[...].reshape(groups * n, 128).T
    columns = [entries[t * KRYLOV : (t + 1) * KRYLOV, :] for t in range(KRYLOV - 1)]
    norms = entries[64:65, :]
    metric = entries[72:80, :]
    sub = lax.broadcasted_iota(jnp.int32, (KRYLOV, 128), 0)
    lanes = lax.broadcasted_iota(jnp.int32, (KRYLOV, 128), 1)
    vectors = [jnp.where(sub == 0, norms / jnp.sqrt(total(norms * norms) + EPS), 0.0)]
    duals = [vectors[0] * metric]
    hess = jnp.zeros((KRYLOV, 128), F32)

    def advance(t, hess):
        now = vectors[t]
        applied = columns[0] * now[0:1, :]
        for i in range(1, t + 1):
            applied = applied + columns[i] * now[i : i + 1, :]
        heights = [total(duals[j] * applied) for j in range(t + 1)]
        for j in range(t + 1):
            hess = jnp.where((sub == j) & (lanes == t), heights[j], hess)
        if t + 1 < KRYLOV:
            rest = applied
            for j in range(t + 1):
                rest = rest - heights[j] * vectors[j]
            beta = jnp.sqrt(total(rest * rest * metric) + EPS)
            hess = jnp.where((sub == t + 1) & (lanes == t), beta, hess)
            vectors.append(rest / beta)
            duals.append(vectors[t + 1] * metric)
        return hess

    for t in range(KRYLOV - 1):
        hess = advance(t, hess)
    for k in range(1, near):
        first_near(k, place).wait_send()
        last_near(k, place).wait_send()
    for k in range(1, lines):
        first_far(k, home).wait_send()
        last_far(k, home).wait_send()
    for k in range(1, lines):
        last_far(k, lax.rem(home + k, lines)).wait_recv()
    columns.append(last_table[...].reshape(groups * n, 128).T[56:64, :])
    hess = advance(KRYLOV - 1, hess)
    hess_ref[...] = hess[:, :KRYLOV]

    scaled = (-TAU / 16.0) * hess
    unit = jnp.where(sub == lanes, 1.0, 0.0).astype(F32)
    second = multiply(scaled, scaled)
    third = multiply(second, scaled)
    inverse = [1.0 / math.factorial(order) for order in range(11)]
    series = inverse[9] * unit + inverse[10] * scaled
    for order in (6, 3, 0):
        lower = inverse[order] * unit + inverse[order + 1] * scaled + inverse[order + 2] * second
        series = lower + multiply(third, series)
    for _ in range(4):
        series = multiply(series, series)
    coefficients = series[:, 0:1]
    length = float(groups * n * block * wide)
    rescale = jnp.sqrt(jnp.full((1, 1), length, F32)) / jnp.sqrt(
        jnp.sum(coefficients * coefficients, axis=0, keepdims=True)
    )
    mixed = coefficients[0:1, :] * vectors[0]
    for t in range(1, KRYLOV):
        mixed = mixed + coefficients[t : t + 1, :] * vectors[t]
    weight = jnp.sum(jnp.where(lanes == group * n + me, mixed, 0.0), axis=1, keepdims=True) * rescale
    for p in range(phys):
        columns_p = slice(p * block, (p + 1) * block)
        acc = weight[0:1, :] * basis[0, :, columns_p]
        for j in range(1, KRYLOV):
            acc = acc + weight[j : j + 1, :] * basis[j, :, columns_p]
        out_ref[:, p, :] = acc


def finish_kernel(state_in, matrix_in, state_out, matrix_out, sems):
    copies = [
        pltpu.make_async_copy(state_in, state_out, sems.at[0]),
        pltpu.make_async_copy(matrix_in, matrix_out, sems.at[1]),
    ]
    for copy in copies:
        copy.start()
    for copy in copies:
        copy.wait()


def local(state, panel, left_env, right_env, left_match, right_match, phys_states):
    n, groups = lax.axis_size("sector"), lax.axis_size("group")
    channels, block = left_env.shape[1], left_env.shape[2]
    phys = phys_states.shape[1]
    wide = phys * block
    rows = state.reshape(-1, state.shape[-1])
    vmem = pl.BlockSpec(memory_space=pltpu.VMEM)
    whole = pl.BlockSpec(memory_space=pl.ANY)
    piece = (n, block, block)
    matches = (left_match * n + right_match).reshape(1, 1)
    dma = pltpu.SemaphoreType.DMA
    parts, matrix = pl.pallas_call(
        kernel,
        out_shape=(
            jax.ShapeDtypeStruct(state.shape[1:], F32),
            jax.ShapeDtypeStruct((KRYLOV, KRYLOV), F32),
        ),
        in_specs=[whole] * 6,
        out_specs=(vmem, vmem),
        scratch_shapes=[
            pltpu.SMEM((1, 1), jnp.int32),
            pltpu.SMEM(phys_states.shape, jnp.int32),
            pltpu.VMEM(rows.shape, F32),
            pltpu.VMEM(piece, BF16),
            pltpu.VMEM(piece, BF16),
            pltpu.VMEM(piece, BF16),
            pltpu.VMEM(piece, BF16),
            pltpu.VMEM(piece, BF16),
            pltpu.VMEM(piece, BF16),
            pltpu.VMEM(piece, BF16),
            pltpu.VMEM(piece, BF16),
            pltpu.VMEM((n, 1, 128), jnp.int32),
            pltpu.SMEM((n, 1, 128), jnp.int32),
            pltpu.VMEM((groups,) + panel.shape, BF16),
            pltpu.VMEM((phys * phys, channels * channels), F32),
            pltpu.VMEM((phys, channels * phys * 8, channels * 8), BF16),
            pltpu.VMEM((channels * phys, block, wide), BF16),
            pltpu.VMEM((block, channels * block), BF16),
            pltpu.VMEM((channels, block, wide), BF16),
            pltpu.VMEM((block, wide), BF16),
            pltpu.VMEM((block, wide), F32),
            pltpu.VMEM((KRYLOV, block, wide), F32),
            pltpu.VMEM((KRYLOV, 128), F32),
            pltpu.VMEM((1, 128), F32),
            pltpu.VMEM((1, 128), F32),
            pltpu.VMEM((groups * SIDE, 2 * SIDE, 128), F32),
            pltpu.VMEM((groups * SIDE, 2 * SIDE, 128), F32),
            dma((8,)),
        ]
        + [dma((n,))] * 10
        + [dma((groups,))] * 2
        + [dma((2 * SIDE,))] * 2
        + [dma((groups * SIDE,))] * 2
        + [dma((2 * SIDE,))] * 2
        + [dma((groups * SIDE,))] * 2,
        compiler_params=pltpu.CompilerParams(collective_id=0, has_side_effects=True, vmem_limit_bytes=VMEM_LIMIT),
        name="step",
    )(matches, phys_states, rows, panel, left_env[0], right_env[0])
    new_state, hessenberg = pl.pallas_call(
        finish_kernel,
        out_shape=(
            jax.ShapeDtypeStruct(state.shape[1:], F32),
            jax.ShapeDtypeStruct((KRYLOV, KRYLOV), F32),
        ),
        in_specs=[vmem, vmem],
        out_specs=(whole, whole),
        scratch_shapes=[dma((2,))],
        name="finish",
    )(parts, matrix)
    return new_state.reshape(state.shape), hessenberg


def solution(mesh):
    return jax.shard_map(
        local,
        mesh=mesh,
        in_specs=(
            P(("group", "sector"), None, None, None),
            P("group", None, None),
            P(("group", "sector"), None, None, None),
            P(("group", "sector"), None, None, None),
            P(("group", "sector")),
            P(("group", "sector")),
            P(("group", "sector"), None),
        ),
        out_specs=(P(("group", "sector"), None, None, None), P()),
        check_vma=False,
    )
```
